128 devices in a mesh: lat: 16 (over y, z_lo, core), lon: 8 (over x, z_hi).
Axes of the slice: x: 4, y: 4, z: 4 (z_hi: 2, z_lo: 2; z = z_hi * 2 + z_lo), core: 2. Of those that a mesh axis runs over, the one named last changes fastest.
Arguments:
- tokens: float32 [256, 512, 512], P('lat', 'lon'), may hold values from -20 to 20
- fine_gain: float32 [512], replicated, may hold values from 0.1 to 1.9
- fine_qkv: bfloat16 [512, 1536], replicated
- fine_proj: bfloat16 [512, 512], replicated, may hold values from -0.25 to 0.25
- merge_gain: float32 [2048], replicated, may hold values from 0.1 to 1.9
- merge_weight: bfloat16 [2048, 1024], replicated, may hold values from -0.125 to 0.125
- coarse_gain: float32 [1024], replicated, may hold values from 0.1 to 1.9
- coarse_qkv: bfloat16 [1024, 3072], replicated
- coarse_proj: bfloat16 [1024, 1024], replicated, may hold values from -0.1875 to 0.1875
- expand_weight: bfloat16 [1024, 2048], replicated, may hold values from -0.1875 to 0.1875
- cotangent: float32 [256, 512, 512], P('lat', 'lon'), may hold values from -6 to 6
Outputs:
- result: float32 [256, 512, 512], P('lat', 'lon')
- grad_tokens: float32 [256, 512, 512], P('lat', 'lon')
The draws below stay inside these ranges and needn't reach their ends.
All inputs are finite; a program needn't handle non-finite values.
Results may differ from the reference program's by a relative error of at most 0.014.
Values may be sent and summed in bfloat16 or wider, within the bound.
A program may use at most 128 MiB of HBM per device.

```python
import math
import jax
import jax.numpy as jnp
from jax import lax

EMBED = 512
WIDE = 1024
FINE_HEADS = 8
COARSE_HEADS = 16
WINDOW = 8
NLAT = 256
NLON = 512


def qkv_matrix(key, channels):
    base_key = jax.random.fold_in(key, 0)
    base_draw = jax.random.truncated_normal(base_key, -4.0, 4.0, (channels, 3 * channels), jnp.float32) / math.sqrt(channels)
    queries = base_draw[:, :channels]
    return jnp.concatenate([queries, base_draw[:, channels:]], axis=1)


def draw_tokens(key, part):
    key = jax.random.fold_in(key, 1)
    noise_key = jax.random.fold_in(key, 0)
    return jax.random.truncated_normal(noise_key, -6.0, 6.0, (NLAT, NLON, EMBED), jnp.float32)


def draw_fine_qkv(key, part):
    key = jax.random.fold_in(key, 2)
    return qkv_matrix(key, EMBED).astype(jnp.bfloat16)


def draw_coarse_qkv(key, part):
    key = jax.random.fold_in(key, 3)
    return qkv_matrix(key, WIDE).astype(jnp.bfloat16)


def block_scale(stream_key, extent, cuts, smallest, largest):
    level, own = 1.0, jax.random.fold_in(stream_key, 6)
    for dim, shards_of in cuts:
        heights = jnp.exp(jax.random.uniform(jax.random.fold_in(own, dim), (shards_of,), jnp.float32, smallest / len(cuts), largest / len(cuts)))
        level = level * jnp.repeat(heights, extent[dim] // shards_of).reshape([-1 if axis == dim else 1 for axis in range(len(extent))])
    return level


def scatter_about(rng, dims, width, limit, pieces=(), dtype=jnp.bfloat16):
    loudness = block_scale(rng, dims, pieces, -0.22, 0.18) if pieces else 1.0
    array = jax.random.normal(rng, dims, jnp.float32) * width * loudness
    return jnp.minimum(jnp.maximum(array, -limit), limit).astype(dtype)


def setup_inputs(seed: int = 0) -> dict:
    seeds = jax.random.split(jax.random.key(seed), 12)
    return {
        "tokens": draw_tokens(jax.random.fold_in(seeds[11], 71), 0),
        "fine_gain": jnp.clip(1.0 + 0.18 * jax.random.normal(seeds[1], (EMBED,), jnp.float32), 0.1, 1.9),
        "fine_qkv": draw_fine_qkv(jax.random.fold_in(seeds[11], 71), 0),
        "fine_proj": scatter_about(seeds[3], (EMBED, EMBED), EMBED ** -0.5, 0.25),
        "merge_gain": jnp.clip(1.0 + 0.18 * jax.random.normal(seeds[4], (4 * EMBED,), jnp.float32), 0.1, 1.9),
        "merge_weight": scatter_about(seeds[5], (4 * EMBED, WIDE), (4 * EMBED) ** -0.5, 0.125),
        "coarse_gain": jnp.clip(1.0 + 0.18 * jax.random.normal(seeds[6], (WIDE,), jnp.float32), 0.1, 1.9),
        "coarse_qkv": draw_coarse_qkv(jax.random.fold_in(seeds[11], 71), 0),
        "coarse_proj": scatter_about(seeds[8], (WIDE, WIDE), WIDE ** -0.5, 0.1875),
        "expand_weight": scatter_about(seeds[9], (WIDE, 4 * EMBED), WIDE ** -0.5, 0.1875),
        "cotangent": scatter_about(seeds[10], (NLAT, NLON, EMBED), 1.0, 6.0, ((0, 16), (1, 8)), jnp.float32),
    }


def layer_norm(grid_field, gain_vec):
    mean_val = lax.optimization_barrier(jnp.mean(grid_field, axis=-1, keepdims=True))
    centred = grid_field - mean_val
    spread = lax.optimization_barrier(jnp.mean(jnp.square(centred), axis=-1, keepdims=True))
    return centred * lax.rsqrt(spread + 1e-05) * gain_vec

def window_attention(qkv_all, group_ids, head_count, window_len):
    row_count, col_count, triple = qkv_all.shape
    channels = triple // 3
    head_size = channels // head_count
    blocks = qkv_all.reshape(row_count // window_len, window_len, col_count // window_len, window_len, 3, head_count, head_size)
    blocks = blocks.transpose(4, 0, 2, 5, 1, 3, 6).reshape(3, row_count // window_len, col_count // window_len, head_count, window_len * window_len, head_size)
    queries = blocks[0].astype(jnp.float32)
    keys_in = blocks[1].astype(jnp.float32)
    values_in = blocks[2].astype(jnp.float32)
    scores = jnp.einsum('abhqd,abhkd->abhqk', queries, keys_in) / math.sqrt(head_size)
    labels = jnp.repeat(group_ids.reshape(row_count // window_len, window_len), window_len, axis=1)
    same_group = labels[:, :, None] == labels[:, None, :]
    scores = jnp.where(same_group[:, None, None], scores, -jnp.inf)
    row_max = lax.optimization_barrier(jnp.max(scores, axis=-1, keepdims=True))
    weights = jnp.exp(scores - row_max)
    probabilities = (weights / lax.optimization_barrier(jnp.sum(weights, axis=-1, keepdims=True))).astype(jnp.bfloat16)
    mixed_heads = jnp.einsum('abhqk,abhkd->abhqd', probabilities.astype(jnp.float32), values_in).astype(jnp.bfloat16)
    mixed_heads = mixed_heads.reshape(row_count // window_len, col_count // window_len, head_count, window_len, window_len, head_size)
    return mixed_heads.transpose(0, 3, 1, 4, 2, 5).reshape(row_count, col_count, channels)

def shifted_block(stream, gain_vec, w_qkv, w_out, head_count, window_len):
    row_count, col_count, channels = stream.shape
    offset = window_len // 2
    group_ids = (jnp.arange(row_count) >= row_count - offset).astype(jnp.int32)
    normed = layer_norm(stream, gain_vec).astype(jnp.bfloat16)
    rolled = jnp.roll(normed, (-offset, -offset), axis=(0, 1))
    qkv_all = jnp.dot(rolled.reshape(row_count * col_count, channels), w_qkv, preferred_element_type=jnp.float32).astype(jnp.bfloat16)
    qkv_all = qkv_all.reshape(row_count // window_len, window_len, col_count, 3 * channels)
    band_groups = group_ids.reshape(row_count // window_len, window_len)
    mixed_heads = lax.map(lambda band_pair: window_attention(band_pair[0], band_pair[1], head_count, window_len), (qkv_all, band_groups))
    projected = jnp.dot(mixed_heads.reshape(row_count * col_count, channels), w_out, preferred_element_type=jnp.float32).astype(jnp.bfloat16)
    projected = projected.reshape(row_count, col_count, channels)
    return stream + jnp.roll(projected, (offset, offset), axis=(0, 1)).astype(jnp.float32)

def merge_cells(grid_field):
    row_count, col_count, channels = grid_field.shape
    return grid_field.reshape(row_count // 2, 2, col_count // 2, 2, channels).transpose(0, 2, 1, 3, 4).reshape(row_count // 2, col_count // 2, 4 * channels)

def split_cells(grid_field):
    row_count, col_count, channels = grid_field.shape
    return grid_field.reshape(row_count, col_count, 2, 2, channels // 4).transpose(0, 2, 1, 3, 4).reshape(2 * row_count, 2 * col_count, channels // 4)

def reference(tokens, fine_gain, fine_qkv, fine_proj, merge_gain, merge_weight, coarse_gain, coarse_qkv, coarse_proj, expand_weight, cotangent):

    def forward(stream):
        fine_out = shifted_block(stream, fine_gain, fine_qkv, fine_proj, FINE_HEADS, WINDOW)
        gathered = layer_norm(merge_cells(fine_out), merge_gain).astype(jnp.bfloat16)
        coarse_in = jnp.dot(gathered, merge_weight, preferred_element_type=jnp.float32)
        coarse_out = shifted_block(coarse_in, coarse_gain, coarse_qkv, coarse_proj, COARSE_HEADS, WINDOW)
        lifted = jnp.dot(coarse_out.astype(jnp.bfloat16), expand_weight, preferred_element_type=jnp.float32)
        return fine_out + split_cells(lifted)
    result, backward = jax.vjp(forward, tokens)
    grad_tokens = backward(cotangent)[0]
    return (result, grad_tokens)
```

```python
import functools
import math

import jax
import jax.numpy as jnp
from jax import lax
from jax.experimental import pallas as pl
from jax.experimental.pallas import tpu as pltpu
from jax.sharding import PartitionSpec as P

F32 = jnp.float32
BF16 = jnp.bfloat16
MESH = pl.DeviceIdType.MESH

ROWS, COLS, CH = 16, 64, 512
CROWS, CCOLS, WIDE = 8, 32, 1024
HEAD = 64
GROUP = 256
TILE = 256
EXP_SCALE = math.log2(math.e) / math.sqrt(HEAD)


def dot(a, b):
    return jnp.dot(a, b, preferred_element_type=F32)


def dot_nt(a, b):
    return lax.dot_general(a, b, (((1,), (1,)), ((), ())), preferred_element_type=F32)


def dot_tn(a, b):
    return lax.dot_general(a, b, (((0,), (0,)), ((), ())), preferred_element_type=F32)


def norm_stats(parts, width):
    mean = sum(jnp.sum(p, axis=-1, keepdims=True) for p in parts) * (1.0 / width)
    centred = [p - mean for p in parts]
    spread = sum(jnp.sum(c * c, axis=-1, keepdims=True) for c in centred) * (1.0 / width)
    return centred, lax.rsqrt(spread + 1e-05)


def norm_grad(parts, grads, gains, width):
    centred, scale = norm_stats(parts, width)
    xhat = [c * scale for c in centred]
    gy = [d * g for d, g in zip(grads, gains)]
    first = sum(jnp.sum(y, axis=-1, keepdims=True) for y in gy) * (1.0 / width)
    second = sum(jnp.sum(y * x, axis=-1, keepdims=True) for y, x in zip(gy, xhat)) * (1.0 / width)
    return [scale * (y - first - x * second) for y, x in zip(gy, xhat)]


def block_diagonal(x, halves):
    zero = jnp.zeros((64, 128), BF16)
    rows = []
    for h in range(4):
        piece = x[:, 128 * (h // 2) : 128 * (h // 2) + 128] * halves[h % 2]
        rows.append(jnp.concatenate([piece, zero] if h < 2 else [zero, piece], axis=1))
    return jnp.concatenate(rows, axis=0)


def per_query(weights, values, low):
    out = []
    for t in range(2):
        lanes = slice(128 * t, 128 * t + 128)
        full = dot_tn(weights[:, lanes], values[:, lanes])
        out.append(jnp.where(low, full[:64], full[64:]))
    return jnp.concatenate(out, axis=1)


def attend(q, k, v, bias, halves, low):
    scores = dot_nt(k, block_diagonal(q, halves)) + bias
    top = jnp.max(scores, axis=0, keepdims=True)
    e = jnp.exp2((scores - top) * EXP_SCALE)
    p = e * (1.0 / jnp.sum(e, axis=0, keepdims=True))
    return p, per_query(p.astype(BF16), v, low)


def attend_grad(q, k, v, p, d_out, halves, low):
    d_diag = block_diagonal(d_out, halves)
    dp = dot_nt(v, d_diag)
    dv = dot(p.astype(BF16), d_diag)
    weighted = p * dp
    ds = ((weighted - p * jnp.sum(weighted, axis=0, keepdims=True)) * (1.0 / math.sqrt(HEAD))).astype(BF16)
    dk = dot(ds, block_diagonal(q, halves))
    dq = per_query(ds, k, low)
    return dq, dk, dv


def aligned(i, step):
    return pl.ds(pl.multiple_of(i * step, step), step)


def kernel(
    tokens, cot, fine_gain, merge_gain, coarse_gain,
    fine_qkv, fine_proj, merge_w, coarse_qkv, coarse_proj, expand_w,
    result, grad,
    tok, cotx, xs, fo, gt, cin, gci, co, xc, gf, res,
    qkv_f, p_f, qkv_c, p_c, n_f, m_f, cells, n_c, m_c, dco, bias,
    w_fq, w_fp, w_m, w_cq, w_cp, w_e,
    load_sem, send_sem, recv_sem,
):
    lat, lon = lax.axis_index("lat"), lax.axis_index("lon")
    n_lat, n_lon = lax.axis_size("lat"), lax.axis_size("lon")
    up, down = lax.rem(lat + n_lat - 1, n_lat), lax.rem(lat + 1, n_lat)
    west, east = lax.rem(lon + n_lon - 1, n_lon), lax.rem(lon + 1, n_lon)

    loads = {}
    for i, (name, src, dst) in enumerate([
        ("tok", tokens, tok.at[0:ROWS, 0:COLS]),
        ("fq", fine_qkv, w_fq),
        ("cot0", cot.at[:, :, 0:128], cotx.at[0:ROWS, 0, 0:COLS]),
        ("cot1", cot.at[:, :, 128:256], cotx.at[0:ROWS, 1, 0:COLS]),
        ("cot2", cot.at[:, :, 256:384], cotx.at[0:ROWS, 2, 0:COLS]),
        ("cot3", cot.at[:, :, 384:512], cotx.at[0:ROWS, 3, 0:COLS]),
        ("e", expand_w, w_e),
        ("fp", fine_proj, w_fp),
        ("m", merge_w, w_m),
        ("cq", coarse_qkv, w_cq),
        ("cp", coarse_proj, w_cp),
    ]):
        loads[name] = pltpu.make_async_copy(src, dst, load_sem.at[i])
        loads[name].start()

    barrier = pltpu.get_barrier_semaphore()
    for a, o in ((up, lon), (lat, west), (up, west), (down, lon), (lat, east), (down, east)):
        pl.semaphore_signal(barrier, inc=1, device_id={"lat": a, "lon": o}, device_id_type=MESH)
    pl.semaphore_wait(barrier, 6)

    def exchange(first, pairs, ahead):
        targets = ((up, lon), (lat, west), (up, west)) if ahead else ((down, lon), (lat, east), (down, east))
        copies = []
        for i, ((src, dst), (a, o)) in enumerate(zip(pairs, targets)):
            copies.append(pltpu.make_async_remote_copy(
                src_ref=src, dst_ref=dst, send_sem=send_sem.at[first + i], recv_sem=recv_sem.at[first + i],
                device_id={"lat": a, "lon": o}, device_id_type=MESH))
            copies[-1].start()
        return copies

    tok_copies = exchange(0, [
        (tokens.at[0:4], tok.at[16:20, 0:64]),
        (tokens.at[:, 0:8], tok.at[0:16, 64:72]),
        (tokens.at[0:4, 0:8], tok.at[16:20, 64:72]),
    ], True)
    for j in range(4):
        loads["cot%d" % j].wait()
    cot_copies = exchange(3, [
        (cotx.at[0:8, :, 0:64], cotx.at[16:24, :, 0:64]),
        (cotx.at[0:16, :, 0:8], cotx.at[0:16, :, 64:72]),
        (cotx.at[0:8, :, 0:8], cotx.at[16:24, :, 64:72]),
    ], True)

    lane = lax.broadcasted_iota(jnp.int32, (1, 128), 1)
    low = lane < 64
    halves = [low.astype(F32).astype(BF16), (lane >= 64).astype(F32).astype(BF16)]
    keys = lax.broadcasted_iota(jnp.int32, (64, GROUP), 0) // 32
    queries = (lax.broadcasted_iota(jnp.int32, (64, GROUP), 1) // 32) % 2
    last = jnp.where(lat == n_lat - 1, 1, 0)
    bias[0] = jnp.zeros((64, GROUP), F32)
    bias[1] = jnp.where((keys != queries) & (last == 1), -jnp.inf, 0.0)

    def product(a, w, tiles, put):
        def step(n, carry):
            put(n, dot(a, w[:, aligned(n, TILE)]))
            return carry
        lax.fori_loop(0, tiles, step, 0)

    def product_t(a, w, tiles, put):
        def step(n, carry):
            put(n, dot_nt(a, w[aligned(n, TILE), :]))
            return carry
        lax.fori_loop(0, tiles, step, 0)

    def store_to(ref, rows):
        def put(n, value):
            ref[rows, aligned(n, TILE)] = value.astype(ref.dtype)
        return put

    def attention(qkv, p_ref, out, first, windows, channels, bias_of):
        groups = channels // GROUP
        def step(w, carry):
            rows = aligned(first + w, 64)
            done = []
            for g in range(groups):
                q, k, v = (qkv[rows, c * channels + g * GROUP : c * channels + (g + 1) * GROUP] for c in range(3))
                done.append(attend(q, k, v, bias[bias_of], halves, low))
            for g, (p, o) in enumerate(done):
                p_ref[rows, g * GROUP : (g + 1) * GROUP] = p
                out[rows, g * GROUP : (g + 1) * GROUP] = o.astype(BF16)
            return carry
        lax.fori_loop(0, windows, step, 0)

    def attention_grad(qkv, p_ref, d_out, first, windows, channels):
        groups = channels // GROUP
        def step(w, carry):
            rows = aligned(first + w, 64)
            done = []
            for g in range(groups):
                lanes = slice(g * GROUP, (g + 1) * GROUP)
                q, k, v = (qkv[rows, c * channels + g * GROUP : c * channels + (g + 1) * GROUP] for c in range(3))
                done.append(attend_grad(q, k, v, p_ref[rows, lanes], d_out[rows, lanes], halves, low))
            for g, grads in enumerate(done):
                for c in range(3):
                    qkv[rows, c * channels + g * GROUP : c * channels + (g + 1) * GROUP] = grads[c].astype(BF16)
            return carry
        lax.fori_loop(0, windows, step, 0)

    def shift_rows(first, count):
        def step(i, carry):
            r = first + i
            xs[r] = tok[r + 4, 4:68, :]
            return carry
        lax.fori_loop(0, count, step, 0)

    def fine_forward(wr):
        def normed(w, carry):
            x = xs[8 * wr : 8 * wr + 8, aligned(w, 8), :].reshape(64, CH)
            (c,), scale = norm_stats([x], CH)
            n_f[aligned(8 * wr + w, 64), :] = (c * scale * fine_gain[...]).astype(BF16)
            return carry
        lax.fori_loop(0, 8, normed, 0)
        half = pl.ds(512 * wr, 512)
        product(n_f[half, :], w_fq, 3 * CH // TILE, store_to(qkv_f, half))
        attention(qkv_f, p_f, m_f, 8 * wr, 8, CH, wr)
        def put(n, value):
            branch = value.astype(BF16).astype(F32)
            lanes = aligned(n, TILE)
            for w in range(8):
                x = xs[8 * wr : 8 * wr + 8, 8 * w : 8 * w + 8, lanes]
                full = x + branch[64 * w : 64 * w + 64].reshape(8, 8, TILE)
                for j in range(2):
                    fo[4 + 8 * wr : 12 + 8 * wr, 2 * n + j, 8 + 8 * w : 16 + 8 * w, :] = full[:, :, 128 * j : 128 * j + 128]
        product(m_f[half, :], w_fp, CH // TILE, put)

    def spread(ref, row, start, count):
        return jnp.concatenate([ref[row, j, pl.ds(start, count, stride=2), :] for j in range(4)], axis=1)

    def merged(i):
        return [spread(fo, 4 + 2 * i + a, 8 + b, 32) for a in range(2) for b in range(2)]

    def merge_forward(wr):
        def normed(i, carry):
            i = 4 * wr + i
            parts, scale = norm_stats(merged(i), 4 * CH)
            for j, c in enumerate(parts):
                gain = merge_gain[:, CH * j : CH * (j + 1)]
                cells[aligned(i, 32), CH * j : CH * (j + 1)] = (c * scale * gain).astype(BF16)
            return carry
        lax.fori_loop(0, 4, normed, 0)
        def put(n, value):
            cin[4 * wr : 4 * wr + 4, 0:32, aligned(n, TILE)] = value.reshape(4, 32, TILE)
        product(cells[128 * wr : 128 * wr + 128, :], w_m, WIDE // TILE, put)

    loads["tok"].wait()
    tok_copies[1].wait_recv()
    shift_rows(0, 12)
    loads["fq"].wait()
    loads["fp"].wait()
    fine_forward(0)
    loads["m"].wait()
    merge_forward(0)
    cin_copies = exchange(6, [(cin.at[0:2, 0:32], cin.at[8:10, 0:32])], True)
    tok_copies[0].wait_recv()
    tok_copies[2].wait_recv()
    shift_rows(12, 4)
    fine_forward(1)
    fo_copies = exchange(9, [
        (fo.at[16:20, :, 8:72], fo.at[0:4, :, 8:72]),
        (fo.at[4:16, :, 64:72], fo.at[4:16, :, 0:8]),
        (fo.at[16:20, :, 64:72], fo.at[0:4, :, 0:8]),
    ], False)
    merge_forward(1)
    cin_copies += [
        pltpu.make_async_remote_copy(
            src_ref=src, dst_ref=dst, send_sem=send_sem.at[7 + i], recv_sem=recv_sem.at[7 + i],
            device_id={"lat": a, "lon": west}, device_id_type=MESH)
        for i, (src, dst, a) in enumerate([
            (cin.at[2:8, 0:8], cin.at[2:8, 32:40], lat),
            (cin.at[0:2, 0:8], cin.at[8:10, 32:40], up),
        ])
    ]
    for c in cin_copies[1:]:
        c.start()

    for c in cot_copies:
        c.wait_recv()
    def gather_cot(i, carry):
        for w in range(4):
            for a in range(2):
                for b in range(2):
                    both = [spread(cotx, 8 + 4 * i + 2 * e + a, 8 + 16 * w + b, 8) for e in range(2)]
                    part = 2 * a + b
                    cells[pl.ds(pl.multiple_of(64 * w + 16 * i, 16), 16), CH * part : CH * (part + 1)] = jnp.concatenate(both, axis=0).astype(BF16)
        return carry
    lax.fori_loop(0, 4, gather_cot, 0)
    loads["e"].wait()
    everything = slice(0, 256)
    product_t(cells[...], w_e, WIDE // TILE, store_to(dco, everything))

    for c in cin_copies:
        c.wait_recv()
    for w in range(4):
        x = cin[2:10, 2 + 8 * w : 10 + 8 * w, :].reshape(64, WIDE)
        xc[64 * w : 64 * w + 64, :] = x
        (c,), scale = norm_stats([x], WIDE)
        n_c[64 * w : 64 * w + 64, :] = (c * scale * coarse_gain[...]).astype(BF16)
    loads["cq"].wait()
    product(n_c[...], w_cq, 3 * WIDE // TILE, store_to(qkv_c, everything))
    attention(qkv_c, p_c, m_c, 0, 4, WIDE, 1)
    loads["cp"].wait()
    def put_co(n, value):
        lanes = aligned(n, TILE)
        full = xc[:, lanes] + value.astype(BF16).astype(F32)
        for w in range(4):
            co[4:12, 8 + 8 * w : 16 + 8 * w, lanes] = full[64 * w : 64 * w + 64].reshape(8, 8, TILE)
    product(m_c[...], w_cp, WIDE // TILE, put_co)
    co_copies = exchange(12, [
        (co.at[8:12, 8:40], co.at[0:4, 8:40]),
        (co.at[4:8, 32:40], co.at[4:8, 0:8]),
        (co.at[8:12, 32:40], co.at[0:4, 0:8]),
    ], False)

    product_t(dco[...], w_cp, WIDE // TILE, store_to(m_c, everything))
    attention_grad(qkv_c, p_c, m_c, 0, 4, WIDE)
    product_t(qkv_c[...], w_cq, WIDE // TILE, store_to(n_c, everything))
    for w in range(4):
        rows = slice(64 * w, 64 * w + 64)
        (d,) = norm_grad([xc[rows, :]], [n_c[rows, :].astype(F32)], [coarse_gain[...]], WIDE)
        gci[2:10, 8 + 8 * w : 16 + 8 * w, :] = (d + dco[rows, :].astype(F32)).reshape(8, 8, WIDE)
    gci_copies = exchange(15, [
        (gci.at[8:10, 8:40], gci.at[0:2, 8:40]),
        (gci.at[2:8, 32:40], gci.at[2:8, 0:8]),
        (gci.at[8:10, 32:40], gci.at[0:2, 0:8]),
    ], False)

    for c in co_copies + fo_copies:
        c.wait_recv()
    for i in range(8):
        n_c[32 * i : 32 * i + 32, :] = co[i, 4:36, :].astype(BF16)
    for a in range(2):
        for b in range(2):
            part = 2 * a + b
            def lift(n, carry):
                w = w_e[:, pl.ds(pl.multiple_of(part * CH + n * TILE, TILE), TILE)]
                lifted = dot(n_c[...], w)
                for s in range(2):
                    j = 2 * n + s
                    for i in range(8):
                        part_fo = fo[2 * i + a, j, pl.ds(4 + b, 32, stride=2), :]
                        res[2 * i + a, j, pl.ds(b, 32, stride=2), :] = part_fo + lifted[32 * i : 32 * i + 32, 128 * s : 128 * s + 128]
                return carry
            lax.fori_loop(0, CH // TILE, lift, 0)
    out_result = [
        pltpu.make_async_copy(res.at[:, j], result.at[:, :, 128 * j : 128 * j + 128], load_sem.at[11 + j])
        for j in range(4)
    ]
    for c in out_result:
        c.start()

    for c in gci_copies:
        c.wait_recv()
    for i in range(8):
        n_c[32 * i : 32 * i + 32, :] = gci[i, 6:38, :].astype(BF16)
    product_t(n_c[...], w_m, 4 * CH // TILE, store_to(cells, everything))
    def merge_grad(i, carry):
        gains = [merge_gain[:, CH * j : CH * (j + 1)] for j in range(4)]
        grads = [cells[aligned(i, 32), CH * j : CH * (j + 1)].astype(F32) for j in range(4)]
        done = norm_grad(merged(i), grads, gains, 4 * CH)
        for a in range(2):
            for b in range(2):
                full = spread(cotx, 4 + 2 * i + a, 4 + b, 32) + done[2 * a + b]
                for j in range(4):
                    gf[2 * i + a, j, pl.ds(b, 32, stride=2), :] = full[:, 128 * j : 128 * j + 128]
        return carry
    lax.fori_loop(0, 8, merge_grad, 0)

    def window(wr, w):
        return jnp.concatenate(
            [gf[8 * wr : 8 * wr + 8, j, aligned(w, 8), :].reshape(64, 128) for j in range(4)], axis=1)
    def to_windows(w, carry):
        for wr in range(2):
            n_f[aligned(8 * wr + w, 64), :] = window(wr, w).astype(BF16)
        return carry
    def fine_grad(wr):
        half = pl.ds(512 * wr, 512)
        product_t(n_f[half, :], w_fp, CH // TILE, store_to(m_f, half))
        attention_grad(qkv_f, p_f, m_f, 8 * wr, 8, CH)
        product_t(qkv_f[half, :], w_fq, CH // TILE, store_to(n_f, half))
        def finish(w, carry):
            cols = aligned(w, 8)
            x = xs[8 * wr : 8 * wr + 8, cols, :].reshape(64, CH)
            dn = n_f[aligned(8 * wr + w, 64), :].astype(F32)
            (d,) = norm_grad([x], [dn], [fine_gain[...]], CH)
            full = (window(wr, w) + d).reshape(8, 8, CH)
            gt[4 + 8 * wr : 12 + 8 * wr, pl.ds(pl.multiple_of(8 + 8 * w, 8), 8), :] = full
            return carry
        lax.fori_loop(0, 8, finish, 0)
    lax.fori_loop(0, 8, to_windows, 0)
    fine_grad(1)
    gt_copies = exchange(18, [(gt.at[16:20, 8:72], gt.at[0:4, 8:72])], False)
    fine_grad(0)
    gt_copies += [
        pltpu.make_async_remote_copy(
            src_ref=src, dst_ref=dst, send_sem=send_sem.at[19 + i], recv_sem=recv_sem.at[19 + i],
            device_id={"lat": a, "lon": east}, device_id_type=MESH)
        for i, (src, dst, a) in enumerate([
            (gt.at[4:16, 64:72], gt.at[4:16, 0:8], lat),
            (gt.at[16:20, 64:72], gt.at[0:4, 0:8], down),
        ])
    ]
    for c in gt_copies[1:]:
        c.start()
    for c in gt_copies:
        c.wait_recv()
    def finish_rows(i, carry):
        xs[i] = gt[i, 4:68, :]
        return carry
    lax.fori_loop(0, ROWS, finish_rows, 0)
    out_grad = pltpu.make_async_copy(xs, grad, load_sem.at[15])
    out_grad.start()
    for c in tok_copies + cot_copies + cin_copies + fo_copies + co_copies + gci_copies + gt_copies:
        c.wait_send()
    for c in out_result + [out_grad]:
        c.wait()


def local(
    tokens, fine_gain, fine_qkv, fine_proj, merge_gain, merge_weight,
    coarse_gain, coarse_qkv, coarse_proj, expand_weight, cotangent,
):
    vmem = pltpu.VMEM
    shape = jax.ShapeDtypeStruct((ROWS, COLS, CH), F32)
    hbm = pl.BlockSpec(memory_space=pl.ANY)
    whole = pl.BlockSpec(memory_space=pltpu.VMEM)
    return pl.pallas_call(
        kernel,
        out_shape=(shape, shape),
        in_specs=[hbm, hbm, whole, whole, whole] + [hbm] * 6,
        out_specs=(hbm, hbm),
        scratch_shapes=[
            vmem((20, 72, CH), F32),
            vmem((24, 4, 72, 128), F32),
            vmem((ROWS, COLS, CH), F32),
            vmem((20, 4, 72, 128), F32),
            vmem((20, 72, CH), F32),
            vmem((10, 40, WIDE), F32),
            vmem((10, 40, WIDE), F32),
            vmem((12, 40, WIDE), F32),
            vmem((256, WIDE), F32),
            vmem((ROWS, 4, COLS, 128), F32),
            vmem((ROWS, 4, COLS, 128), F32),
            vmem((1024, 3 * CH), BF16),
            vmem((1024, CH), F32),
            vmem((256, 3 * WIDE), BF16),
            vmem((256, WIDE), F32),
            vmem((1024, CH), BF16),
            vmem((1024, CH), BF16),
            vmem((256, 4 * CH), BF16),
            vmem((256, WIDE), BF16),
            vmem((256, WIDE), BF16),
            vmem((256, WIDE), BF16),
            vmem((2, 64, GROUP), F32),
            vmem(fine_qkv.shape, BF16),
            vmem(fine_proj.shape, BF16),
            vmem(merge_weight.shape, BF16),
            vmem(coarse_qkv.shape, BF16),
            vmem(coarse_proj.shape, BF16),
            vmem(expand_weight.shape, BF16),
            pltpu.SemaphoreType.DMA((16,)),
            pltpu.SemaphoreType.DMA((21,)),
            pltpu.SemaphoreType.DMA((21,)),
        ],
        compiler_params=pltpu.CompilerParams(
            collective_id=0, has_side_effects=True, vmem_limit_bytes=63 * 1024 * 1024),
    )(
        tokens, cotangent, fine_gain.reshape(1, -1), merge_gain.reshape(1, -1), coarse_gain.reshape(1, -1),
        fine_qkv, fine_proj, merge_weight, coarse_qkv, coarse_proj, expand_weight,
    )


def solution(mesh):
    field = P("lat", "lon", None)
    placed = (field,) + (P(),) * 9 + (field,)
    return jax.shard_map(local, mesh=mesh, in_specs=placed, out_specs=(field, field), check_vma=False)
```

```python
import functools
import math

import jax
import jax.numpy as jnp
from jax import lax
from jax.experimental import pallas as pl
from jax.experimental.pallas import tpu as pltpu
from jax.sharding import PartitionSpec as P

F32 = jnp.float32
BF16 = jnp.bfloat16
MESH = pl.DeviceIdType.MESH

ROWS, COLS, CH = 16, 64, 512
CROWS, CCOLS, WIDE = 8, 32, 1024
HEAD = 64
GROUP = 256
TILE = 256
EXP_SCALE = math.log2(math.e) / math.sqrt(HEAD)


def dot(a, b):
    return jnp.dot(a, b, preferred_element_type=F32)


def dot_nt(a, b):
    return lax.dot_general(a, b, (((1,), (1,)), ((), ())), preferred_element_type=F32)


def dot_tn(a, b):
    return lax.dot_general(a, b, (((0,), (0,)), ((), ())), preferred_element_type=F32)


def norm_stats(parts, width):
    mean = sum(jnp.sum(p, axis=-1, keepdims=True) for p in parts) * (1.0 / width)
    centred = [p - mean for p in parts]
    spread = sum(jnp.sum(c * c, axis=-1, keepdims=True) for c in centred) * (1.0 / width)
    return centred, lax.rsqrt(spread + 1e-05)


def norm_grad(parts, grads, gains, width):
    centred, scale = norm_stats(parts, width)
    xhat = [c * scale for c in centred]
    gy = [d * g for d, g in zip(grads, gains)]
    first = sum(jnp.sum(y, axis=-1, keepdims=True) for y in gy) * (1.0 / width)
    second = sum(jnp.sum(y * x, axis=-1, keepdims=True) for y, x in zip(gy, xhat)) * (1.0 / width)
    return [scale * (y - first - x * second) for y, x in zip(gy, xhat)]


def block_diagonal(x, halves):
    zero = jnp.zeros((64, 128), BF16)
    rows = []
    for h in range(4):
        piece = x[:, 128 * (h // 2) : 128 * (h // 2) + 128] * halves[h % 2]
        rows.append(jnp.concatenate([piece, zero] if h < 2 else [zero, piece], axis=1))
    return jnp.concatenate(rows, axis=0)


def per_query(weights, values, low):
    out = []
    for t in range(2):
        lanes = slice(128 * t, 128 * t + 128)
        full = dot_tn(weights[:, lanes], values[:, lanes])
        out.append(jnp.where(low, full[:64], full[64:]))
    return jnp.concatenate(out, axis=1)


def attend(items, bias, halves, low):
    scores = [dot_nt(k, block_diagonal(q, halves)) + bias for q, k, v in items]
    probs = []
    for s in scores:
        e = jnp.exp2((s - jnp.max(s, axis=0, keepdims=True)) * EXP_SCALE)
        probs.append(e * (1.0 / jnp.sum(e, axis=0, keepdims=True)))
    return [(p, per_query(p.astype(BF16), v, low)) for p, (q, k, v) in zip(probs, items)]


def attend_grad(items, probs, d_outs, halves, low):
    d_diags = [block_diagonal(d, halves) for d in d_outs]
    dps = [dot_nt(v, d) for (q, k, v), d in zip(items, d_diags)]
    dvs = [dot(p.astype(BF16), d) for p, d in zip(probs, d_diags)]
    dss = []
    for p, dp in zip(probs, dps):
        weighted = p * dp
        dss.append(((weighted - p * jnp.sum(weighted, axis=0, keepdims=True)) * (1.0 / math.sqrt(HEAD))).astype(BF16))
    dks = [dot(ds, block_diagonal(q, halves)) for ds, (q, k, v) in zip(dss, items)]
    dqs = [per_query(ds, k, low) for ds, (q, k, v) in zip(dss, items)]
    return list(zip(dqs, dks, dvs))


def aligned(i, step):
    return pl.ds(i * step, step)


def unrolled(first, last, step):
    for i in range(first, last):
        step(i, 0)


def kernel(
    tokens, cot, fine_gain, merge_gain, coarse_gain,
    fine_qkv, fine_proj, merge_w, coarse_qkv, coarse_proj, expand_w,
    result, grad,
    tok, cotx, xs, fo, gt, cin, gci, co, xc, gf, res,
    qkv_f, p_f, qkv_c, p_c, n_f, m_f, cells, n_c, m_c, dco, bias,
    w_fq, w_fp, w_m, w_cq, w_cp, w_e,
    load_sem, send_sem, recv_sem,
):
    lat, lon = lax.axis_index("lat"), lax.axis_index("lon")
    n_lat, n_lon = lax.axis_size("lat"), lax.axis_size("lon")
    up, down = lax.rem(lat + n_lat - 1, n_lat), lax.rem(lat + 1, n_lat)
    west, east = lax.rem(lon + n_lon - 1, n_lon), lax.rem(lon + 1, n_lon)

    loads = {}
    for i, (name, src, dst) in enumerate([
        ("tok", tokens, tok.at[0:ROWS, 0:COLS]),
        ("fq", fine_qkv, w_fq),
        ("cot0", cot.at[:, :, 0:128], cotx.at[0:ROWS, 0, 0:COLS]),
        ("cot1", cot.at[:, :, 128:256], cotx.at[0:ROWS, 1, 0:COLS]),
        ("cot2", cot.at[:, :, 256:384], cotx.at[0:ROWS, 2, 0:COLS]),
        ("cot3", cot.at[:, :, 384:512], cotx.at[0:ROWS, 3, 0:COLS]),
        ("e", expand_w, w_e),
        ("fp", fine_proj, w_fp),
        ("m", merge_w, w_m),
        ("cq", coarse_qkv, w_cq),
        ("cp", coarse_proj, w_cp),
    ]):
        loads[name] = pltpu.make_async_copy(src, dst, load_sem.at[i])
        loads[name].start()

    barrier = pltpu.get_barrier_semaphore()
    for a, o in ((up, lon), (lat, west), (up, west), (down, lon), (lat, east), (down, east)):
        pl.semaphore_signal(barrier, inc=1, device_id={"lat": a, "lon": o}, device_id_type=MESH)
    pl.semaphore_wait(barrier, 6)

    def exchange(first, pairs, ahead):
        targets = ((up, lon), (lat, west), (up, west)) if ahead else ((down, lon), (lat, east), (down, east))
        copies = []
        for i, ((src, dst), (a, o)) in enumerate(zip(pairs, targets)):
            copies.append(pltpu.make_async_remote_copy(
                src_ref=src, dst_ref=dst, send_sem=send_sem.at[first + i], recv_sem=recv_sem.at[first + i],
                device_id={"lat": a, "lon": o}, device_id_type=MESH))
            copies[-1].start()
        return copies

    tok_copies = exchange(0, [
        (tokens.at[0:4], tok.at[16:20, 0:64]),
        (tokens.at[:, 0:8], tok.at[0:16, 64:72]),
        (tokens.at[0:4, 0:8], tok.at[16:20, 64:72]),
    ], True)
    for j in range(4):
        loads["cot%d" % j].wait()
    cot_copies = exchange(3, [
        (cotx.at[0:8, :, 0:64], cotx.at[16:24, :, 0:64]),
        (cotx.at[0:16, :, 0:8], cotx.at[0:16, :, 64:72]),
        (cotx.at[0:8, :, 0:8], cotx.at[16:24, :, 64:72]),
    ], True)

    lane = lax.broadcasted_iota(jnp.int32, (1, 128), 1)
    low = lane < 64
    halves = [low.astype(F32).astype(BF16), (lane >= 64).astype(F32).astype(BF16)]
    keys = lax.broadcasted_iota(jnp.int32, (64, GROUP), 0) // 32
    queries = (lax.broadcasted_iota(jnp.int32, (64, GROUP), 1) // 32) % 2
    last = jnp.where(lat == n_lat - 1, 1, 0)
    bias[0] = jnp.zeros((64, GROUP), F32)
    bias[1] = jnp.where((keys != queries) & (last == 1), -jnp.inf, 0.0)

    def product(a, w, tiles, put):
        for n in range(tiles):
            put(n, dot(a, w[:, TILE * n : TILE * n + TILE]))

    def product_t(a, w, tiles, put):
        for n in range(tiles):
            put(n, dot_nt(a, w[TILE * n : TILE * n + TILE, :]))

    def store_to(ref, rows):
        def put(n, value):
            ref[rows, TILE * n : TILE * n + TILE] = value.astype(ref.dtype)
        return put

    def groups_of(first, windows, channels):
        for w in range(first, first + windows):
            for g in range(channels // GROUP):
                yield pl.ds(64 * w, 64), [pl.ds(c * channels + g * GROUP, GROUP) for c in range(3)]

    def attention(qkv, p_ref, out, first, windows, channels, bias_of):
        places = list(groups_of(first, windows, channels))
        items = [tuple(qkv[rows, lanes] for lanes in three) for rows, three in places]
        done = attend(items, bias[bias_of], halves, low)
        for (rows, three), (p, o) in zip(places, done):
            p_ref[rows, three[0]] = p
            out[rows, three[0]] = o.astype(BF16)

    def attention_grad(qkv, p_ref, d_out, first, windows, channels):
        places = list(groups_of(first, windows, channels))
        items = [tuple(qkv[rows, lanes] for lanes in three) for rows, three in places]
        probs = [p_ref[rows, three[0]] for rows, three in places]
        d_outs = [d_out[rows, three[0]] for rows, three in places]
        done = attend_grad(items, probs, d_outs, halves, low)
        for (rows, three), grads in zip(places, done):
            for lanes, value in zip(three, grads):
                qkv[rows, lanes] = value.astype(BF16)

    def shift_rows(first, count):
        def step(i, carry):
            r = first + i
            xs[r] = tok[r + 4, 4:68, :]
            return carry
        unrolled(0, count, step)

    def fine_norm(wr):
        def normed(w, carry):
            x = xs[8 * wr : 8 * wr + 8, aligned(w, 8), :].reshape(64, CH)
            (c,), scale = norm_stats([x], CH)
            n_f[aligned(8 * wr + w, 64), :] = (c * scale * fine_gain[...]).astype(BF16)
            return carry
        unrolled(0, 8, normed)
    def fine_expand(wr):
        half = pl.ds(512 * wr, 512)
        product(n_f[half, :], w_fq, 3 * CH // TILE, store_to(qkv_f, half))
    def fine_attend(wr):
        attention(qkv_f, p_f, m_f, 8 * wr, 8, CH, wr)
    def fine_join(wr):
        half = pl.ds(512 * wr, 512)
        def put(n, value):
            branch = value.astype(BF16).astype(F32)
            lanes = aligned(n, TILE)
            for w in range(8):
                x = xs[8 * wr : 8 * wr + 8, 8 * w : 8 * w + 8, lanes]
                full = x + branch[64 * w : 64 * w + 64].reshape(8, 8, TILE)
                for j in range(2):
                    fo[4 + 8 * wr : 12 + 8 * wr, 2 * n + j, 8 + 8 * w : 16 + 8 * w, :] = full[:, :, 128 * j : 128 * j + 128]
        product(m_f[half, :], w_fp, CH // TILE, put)

    def spread(ref, row, start, count):
        return jnp.concatenate([ref[row, j, pl.ds(start, count, stride=2), :] for j in range(4)], axis=1)

    def merged(i):
        return [spread(fo, 4 + 2 * i + a, 8 + b, 32) for a in range(2) for b in range(2)]

    def merge_norm(wr):
        def normed(i, carry):
            i = 4 * wr + i
            parts, scale = norm_stats(merged(i), 4 * CH)
            for j, c in enumerate(parts):
                gain = merge_gain[:, CH * j : CH * (j + 1)]
                cells[aligned(i, 32), CH * j : CH * (j + 1)] = (c * scale * gain).astype(BF16)
            return carry
        unrolled(0, 4, normed)
    def merge_product(wr):
        def put(n, value):
            cin[4 * wr : 4 * wr + 4, 0:32, aligned(n, TILE)] = value.reshape(4, 32, TILE)
        product(cells[128 * wr : 128 * wr + 128, :], w_m, WIDE // TILE, put)

    loads["tok"].wait()
    tok_copies[1].wait_recv()
    shift_rows(0, 12)
    loads["fq"].wait()
    loads["fp"].wait()
    fine_norm(0)
    fine_expand(0)
    fine_attend(0)
    fine_join(0)
    loads["m"].wait()
    merge_norm(0)
    merge_product(0)
    cin_copies = exchange(6, [(cin.at[0:2, 0:32], cin.at[8:10, 0:32])], True)
    tok_copies[0].wait_recv()
    tok_copies[2].wait_recv()
    shift_rows(12, 4)
    fine_norm(1)
    fine_expand(1)
    fine_attend(1)
    fine_join(1)
    fo_copies = exchange(9, [
        (fo.at[16:20, :, 8:72], fo.at[0:4, :, 8:72]),
        (fo.at[4:16, :, 64:72], fo.at[4:16, :, 0:8]),
        (fo.at[16:20, :, 64:72], fo.at[0:4, :, 0:8]),
    ], False)
    merge_norm(1)
    merge_product(1)
    cin_copies += [
        pltpu.make_async_remote_copy(
            src_ref=src, dst_ref=dst, send_sem=send_sem.at[7 + i], recv_sem=recv_sem.at[7 + i],
            device_id={"lat": a, "lon": west}, device_id_type=MESH)
        for i, (src, dst, a) in enumerate([
            (cin.at[2:8, 0:8], cin.at[2:8, 32:40], lat),
            (cin.at[0:2, 0:8], cin.at[8:10, 32:40], up),
        ])
    ]
    for c in cin_copies[1:]:
        c.start()

    for c in cot_copies:
        c.wait_recv()
    def gather_cot(i, carry):
        for w in range(4):
            for a in range(2):
                for b in range(2):
                    both = [spread(cotx, 8 + 4 * i + 2 * e + a, 8 + 16 * w + b, 8) for e in range(2)]
                    part = 2 * a + b
                    cells[pl.ds(64 * w + 16 * i, 16), CH * part : CH * (part + 1)] = jnp.concatenate(both, axis=0).astype(BF16)
        return carry
    unrolled(0, 4, gather_cot)
    loads["e"].wait()
    everything = slice(0, 256)
    product_t(cells[...], w_e, WIDE // TILE, store_to(dco, everything))

    for c in cin_copies:
        c.wait_recv()
    for w in range(4):
        x = cin[2:10, 2 + 8 * w : 10 + 8 * w, :].reshape(64, WIDE)
        xc[64 * w : 64 * w + 64, :] = x
        (c,), scale = norm_stats([x], WIDE)
        n_c[64 * w : 64 * w + 64, :] = (c * scale * coarse_gain[...]).astype(BF16)
    loads["cq"].wait()
    product(n_c[...], w_cq, 3 * WIDE // TILE, store_to(qkv_c, everything))
    attention(qkv_c, p_c, m_c, 0, 4, WIDE, 1)
    loads["cp"].wait()
    def put_co(n, value):
        lanes = aligned(n, TILE)
        full = xc[:, lanes] + value.astype(BF16).astype(F32)
        for w in range(4):
            co[4:12, 8 + 8 * w : 16 + 8 * w, lanes] = full[64 * w : 64 * w + 64].reshape(8, 8, TILE)
    product(m_c[...], w_cp, WIDE // TILE, put_co)
    co_copies = exchange(12, [
        (co.at[8:12, 8:40], co.at[0:4, 8:40]),
        (co.at[4:8, 32:40], co.at[4:8, 0:8]),
        (co.at[8:12, 32:40], co.at[0:4, 0:8]),
    ], False)

    product_t(dco[...], w_cp, WIDE // TILE, store_to(m_c, everything))
    attention_grad(qkv_c, p_c, m_c, 0, 4, WIDE)
    product_t(qkv_c[...], w_cq, WIDE // TILE, store_to(n_c, everything))
    for w in range(4):
        rows = slice(64 * w, 64 * w + 64)
        (d,) = norm_grad([xc[rows, :]], [n_c[rows, :].astype(F32)], [coarse_gain[...]], WIDE)
        gci[2:10, 8 + 8 * w : 16 + 8 * w, :] = (d + dco[rows, :].astype(F32)).reshape(8, 8, WIDE)
    gci_copies = exchange(15, [
        (gci.at[8:10, 8:40], gci.at[0:2, 8:40]),
        (gci.at[2:8, 32:40], gci.at[2:8, 0:8]),
        (gci.at[8:10, 32:40], gci.at[0:2, 0:8]),
    ], False)

    for c in co_copies + fo_copies:
        c.wait_recv()
    for i in range(8):
        n_c[32 * i : 32 * i + 32, :] = co[i, 4:36, :].astype(BF16)
    for a in range(2):
        for b in range(2):
            part = 2 * a + b
            def lift(n, carry):
                w = w_e[:, pl.ds(part * CH + n * TILE, TILE)]
                lifted = dot(n_c[...], w)
                for s in range(2):
                    j = 2 * n + s
                    for i in range(8):
                        part_fo = fo[2 * i + a, j, pl.ds(4 + b, 32, stride=2), :]
                        res[2 * i + a, j, pl.ds(b, 32, stride=2), :] = part_fo + lifted[32 * i : 32 * i + 32, 128 * s : 128 * s + 128]
                return carry
            unrolled(0, CH // TILE, lift)
    out_result = [
        pltpu.make_async_copy(res.at[:, j], result.at[:, :, 128 * j : 128 * j + 128], load_sem.at[11 + j])
        for j in range(4)
    ]
    for c in out_result:
        c.start()

    for c in gci_copies:
        c.wait_recv()
    for i in range(8):
        n_c[32 * i : 32 * i + 32, :] = gci[i, 6:38, :].astype(BF16)
    product_t(n_c[...], w_m, 4 * CH // TILE, store_to(cells, everything))
    def merge_grad(i, carry):
        gains = [merge_gain[:, CH * j : CH * (j + 1)] for j in range(4)]
        grads = [cells[aligned(i, 32), CH * j : CH * (j + 1)].astype(F32) for j in range(4)]
        done = norm_grad(merged(i), grads, gains, 4 * CH)
        for a in range(2):
            for b in range(2):
                full = spread(cotx, 4 + 2 * i + a, 4 + b, 32) + done[2 * a + b]
                for j in range(4):
                    gf[2 * i + a, j, pl.ds(b, 32, stride=2), :] = full[:, 128 * j : 128 * j + 128]
        return carry
    unrolled(0, 8, merge_grad)

    def window(wr, w):
        return jnp.concatenate(
            [gf[8 * wr : 8 * wr + 8, j, aligned(w, 8), :].reshape(64, 128) for j in range(4)], axis=1)
    def to_windows(w, carry):
        for wr in range(2):
            n_f[aligned(8 * wr + w, 64), :] = window(wr, w).astype(BF16)
        return carry
    def fine_grad_a(wr):
        half = pl.ds(512 * wr, 512)
        product_t(n_f[half, :], w_fp, CH // TILE, store_to(m_f, half))
    def fine_grad_b(wr):
        attention_grad(qkv_f, p_f, m_f, 8 * wr, 8, CH)
    def fine_grad_c(wr):
        half = pl.ds(512 * wr, 512)
        product_t(qkv_f[half, :], w_fq, CH // TILE, store_to(n_f, half))
    def fine_grad_d(wr):
        def finish(w, carry):
            cols = aligned(w, 8)
            x = xs[8 * wr : 8 * wr + 8, cols, :].reshape(64, CH)
            dn = n_f[aligned(8 * wr + w, 64), :].astype(F32)
            (d,) = norm_grad([x], [dn], [fine_gain[...]], CH)
            full = (window(wr, w) + d).reshape(8, 8, CH)
            gt[4 + 8 * wr : 12 + 8 * wr, pl.ds(8 + 8 * w, 8), :] = full
            return carry
        unrolled(0, 8, finish)
    unrolled(0, 8, to_windows)
    fine_grad_a(1)
    fine_grad_b(1)
    fine_grad_c(1)
    fine_grad_d(1)
    gt_copies = exchange(18, [(gt.at[16:20, 8:72], gt.at[0:4, 8:72])], False)
    fine_grad_a(0)
    fine_grad_b(0)
    fine_grad_c(0)
    fine_grad_d(0)
    gt_copies += [
        pltpu.make_async_remote_copy(
            src_ref=src, dst_ref=dst, send_sem=send_sem.at[19 + i], recv_sem=recv_sem.at[19 + i],
            device_id={"lat": a, "lon": east}, device_id_type=MESH)
        for i, (src, dst, a) in enumerate([
            (gt.at[4:16, 64:72], gt.at[4:16, 0:8], lat),
            (gt.at[16:20, 64:72], gt.at[0:4, 0:8], down),
        ])
    ]
    for c in gt_copies[1:]:
        c.start()
    for c in gt_copies:
        c.wait_recv()
    def finish_rows(i, carry):
        xs[i] = gt[i, 4:68, :]
        return carry
    unrolled(0, ROWS, finish_rows)
    out_grad = pltpu.make_async_copy(xs, grad, load_sem.at[15])
    out_grad.start()
    for c in tok_copies + cot_copies + cin_copies + fo_copies + co_copies + gci_copies + gt_copies:
        c.wait_send()
    for c in out_result + [out_grad]:
        c.wait()


def local(
    tokens, fine_gain, fine_qkv, fine_proj, merge_gain, merge_weight,
    coarse_gain, coarse_qkv, coarse_proj, expand_weight, cotangent,
):
    vmem = pltpu.VMEM
    shape = jax.ShapeDtypeStruct((ROWS, COLS, CH), F32)
    hbm = pl.BlockSpec(memory_space=pl.ANY)
    whole = pl.BlockSpec(memory_space=pltpu.VMEM)
    return pl.pallas_call(
        kernel,
        out_shape=(shape, shape),
        in_specs=[hbm, hbm, whole, whole, whole] + [hbm] * 6,
        out_specs=(hbm, hbm),
        scratch_shapes=[
            vmem((20, 72, CH), F32),
            vmem((24, 4, 72, 128), F32),
            vmem((ROWS, COLS, CH), F32),
            vmem((20, 4, 72, 128), F32),
            vmem((20, 72, CH), F32),
            vmem((10, 40, WIDE), F32),
            vmem((10, 40, WIDE), F32),
            vmem((12, 40, WIDE), F32),
            vmem((256, WIDE), F32),
            vmem((ROWS, 4, COLS, 128), F32),
            vmem((ROWS, 4, COLS, 128), F32),
            vmem((1024, 3 * CH), BF16),
            vmem((1024, CH), F32),
            vmem((256, 3 * WIDE), BF16),
            vmem((256, WIDE), F32),
            vmem((1024, CH), BF16),
            vmem((1024, CH), BF16),
            vmem((256, 4 * CH), BF16),
            vmem((256, WIDE), BF16),
            vmem((256, WIDE), BF16),
            vmem((256, WIDE), BF16),
            vmem((2, 64, GROUP), F32),
            vmem(fine_qkv.shape, BF16),
            vmem(fine_proj.shape, BF16),
            vmem(merge_weight.shape, BF16),
            vmem(coarse_qkv.shape, BF16),
            vmem(coarse_proj.shape, BF16),
            vmem(expand_weight.shape, BF16),
            pltpu.SemaphoreType.DMA((16,)),
            pltpu.SemaphoreType.DMA((21,)),
            pltpu.SemaphoreType.DMA((21,)),
        ],
        compiler_params=pltpu.CompilerParams(
            collective_id=0, has_side_effects=True, vmem_limit_bytes=63 * 1024 * 1024),
    )(
        tokens, cotangent, fine_gain.reshape(1, -1), merge_gain.reshape(1, -1), coarse_gain.reshape(1, -1),
        fine_qkv, fine_proj, merge_weight, coarse_qkv, coarse_proj, expand_weight,
    )


def solution(mesh):
    field = P("lat", "lon", None)
    placed = (field,) + (P(),) * 9 + (field,)
    return jax.shard_map(local, mesh=mesh, in_specs=placed, out_specs=(field, field), check_vma=False)
```

```python
import functools
import math

import jax
import jax.numpy as jnp
from jax import lax
from jax.experimental import pallas as pl
from jax.experimental.pallas import tpu as pltpu
from jax.sharding import PartitionSpec as P

F32 = jnp.float32
BF16 = jnp.bfloat16
MESH = pl.DeviceIdType.MESH

ROWS, COLS, CH = 16, 64, 512
CROWS, CCOLS, WIDE = 8, 32, 1024
HEAD = 64
GROUP = 256
TILE = 256
EXP_SCALE = math.log2(math.e) / math.sqrt(HEAD)


def dot(a, b):
    return jnp.dot(a, b, preferred_element_type=F32)


def dot_nt(a, b):
    return lax.dot_general(a, b, (((1,), (1,)), ((), ())), preferred_element_type=F32)


def dot_tn(a, b):
    return lax.dot_general(a, b, (((0,), (0,)), ((), ())), preferred_element_type=F32)


def norm_stats(parts, width):
    mean = sum(jnp.sum(p, axis=-1, keepdims=True) for p in parts) * (1.0 / width)
    centred = [p - mean for p in parts]
    spread = sum(jnp.sum(c * c, axis=-1, keepdims=True) for c in centred) * (1.0 / width)
    return centred, lax.rsqrt(spread + 1e-05)


def norm_grad(parts, grads, gains, width):
    centred, scale = norm_stats(parts, width)
    xhat = [c * scale for c in centred]
    gy = [d * g for d, g in zip(grads, gains)]
    first = sum(jnp.sum(y, axis=-1, keepdims=True) for y in gy) * (1.0 / width)
    second = sum(jnp.sum(y * x, axis=-1, keepdims=True) for y, x in zip(gy, xhat)) * (1.0 / width)
    return [scale * (y - first - x * second) for y, x in zip(gy, xhat)]


def block_diagonal(x, halves):
    zero = jnp.zeros((64, 128), BF16)
    rows = []
    for h in range(4):
        piece = x[:, 128 * (h // 2) : 128 * (h // 2) + 128] * halves[h % 2]
        rows.append(jnp.concatenate([piece, zero] if h < 2 else [zero, piece], axis=1))
    return jnp.concatenate(rows, axis=0)


def per_query(weights, values, low):
    out = []
    for t in range(2):
        lanes = slice(128 * t, 128 * t + 128)
        full = dot_tn(weights[:, lanes], values[:, lanes])
        out.append(jnp.where(low, full[:64], full[64:]))
    return jnp.concatenate(out, axis=1)


def attend(items, biases, halves, low):
    scores = [dot_nt(k, block_diagonal(q, halves)) + b for (q, k, v), b in zip(items, biases)]
    probs = []
    for s in scores:
        e = jnp.exp2((s - jnp.max(s, axis=0, keepdims=True)) * EXP_SCALE)
        probs.append(e * (1.0 / jnp.sum(e, axis=0, keepdims=True)))
    return [(p, per_query(p.astype(BF16), v, low)) for p, (q, k, v) in zip(probs, items)]


def attend_grad(items, probs, d_outs, halves, low):
    d_diags = [block_diagonal(d, halves) for d in d_outs]
    dps = [dot_nt(v, d) for (q, k, v), d in zip(items, d_diags)]
    dvs = [dot(p.astype(BF16), d) for p, d in zip(probs, d_diags)]
    dss = []
    for p, dp in zip(probs, dps):
        weighted = p * dp
        dss.append(((weighted - p * jnp.sum(weighted, axis=0, keepdims=True)) * (1.0 / math.sqrt(HEAD))).astype(BF16))
    dks = [dot(ds, block_diagonal(q, halves)) for ds, (q, k, v) in zip(dss, items)]
    dqs = [per_query(ds, k, low) for ds, (q, k, v) in zip(dss, items)]
    return list(zip(dqs, dks, dvs))


def aligned(i, step):
    return pl.ds(i * step, step)


def unrolled(first, last, step):
    for i in range(first, last):
        step(i, 0)


def kernel(
    tokens, cot, fine_gain, merge_gain, coarse_gain,
    fine_qkv, fine_proj, merge_w, coarse_qkv, coarse_proj, expand_w,
    result, grad,
    tok, cotx, xs, fo, cin, gci, co, xc, gf, res,
    qkv_f, p_f, qkv_c, p_c, n_f, m_f, cells, n_c, m_c, dm_c, dco, bias,
    w_fq, w_fp, w_m, w_cq, w_cp, w_e,
    tok_s, tok_d, cot_s, cot_d, cin_s, cin_d, fo_s, fo_d, co_s, co_d, gci_s, gci_d, gt_s, gt_d,
    load_sem, send_sem, recv_sem,
):
    lat, lon = lax.axis_index("lat"), lax.axis_index("lon")
    n_lat, n_lon = lax.axis_size("lat"), lax.axis_size("lon")
    up, down = lax.rem(lat + n_lat - 1, n_lat), lax.rem(lat + 1, n_lat)
    west, east = lax.rem(lon + n_lon - 1, n_lon), lax.rem(lon + 1, n_lon)

    loads = {}
    def load(name, src, dst):
        loads[name] = pltpu.make_async_copy(src, dst, load_sem.at[len(loads)])
        loads[name].start()

    load("tok", tokens, tok.at[0:ROWS, 0:COLS])
    load("fq", fine_qkv, w_fq)
    for j in range(4):
        load("cot%d" % j, cot.at[:, :, 128 * j : 128 * j + 128], cotx.at[0:ROWS, j, 0:COLS])

    barrier = pltpu.get_barrier_semaphore()
    for a, o in ((up, lon), (lat, west), (up, west), (down, lon), (lat, east), (down, east)):
        pl.semaphore_signal(barrier, inc=1, device_id={"lat": a, "lon": o}, device_id_type=MESH)

    def exchange(first, sent, landed, edge, corner, ahead):
        targets = ((up, lon), (lat, west), (up, west)) if ahead else ((down, lon), (lat, east), (down, east))
        sources = (sent[0], sent[1].at[edge[0] : edge[1]], sent[1].at[corner[0] : corner[1]])
        copies = []
        for i, (src, dst, (a, o)) in enumerate(zip(sources, landed, targets)):
            copies.append(pltpu.make_async_remote_copy(
                src_ref=src, dst_ref=dst, send_sem=send_sem.at[first + i], recv_sem=recv_sem.at[first + i],
                device_id={"lat": a, "lon": o}, device_id_type=MESH))
            copies[-1].start()
        return copies

    def pieces(value, start, size):
        return jnp.concatenate([value[8 * a + start : 8 * a + start + size] for a in range(value.shape[0] // 8)], axis=0)

    loads["tok"].wait()
    for i in range(4):
        tok_s[0][i] = tok[i, 0:64, :].astype(BF16)
        tok_s[1][16 * i : 16 * i + 16, :] = jnp.concatenate([tok[4 * i + e, 0:4, :] for e in range(4)], axis=0).astype(BF16)
    pl.semaphore_wait(barrier, 6)
    tok_copies = exchange(0, tok_s, tok_d, (0, 64), (0, 16), True)
    load("fp", fine_proj, w_fp)
    load("m", merge_w, w_m)
    load("e", expand_w, w_e)

    lane = lax.broadcasted_iota(jnp.int32, (1, 128), 1)
    low = lane < 64
    halves = [low.astype(F32).astype(BF16), (lane >= 64).astype(F32).astype(BF16)]
    keys = lax.broadcasted_iota(jnp.int32, (64, GROUP), 0) // 32
    queries = (lax.broadcasted_iota(jnp.int32, (64, GROUP), 1) // 32) % 2
    last = jnp.where(lat == n_lat - 1, 1, 0)
    bias[0] = jnp.zeros((64, GROUP), F32)
    bias[1] = jnp.where((keys != queries) & (last == 1), -jnp.inf, 0.0)

    def product(a, w, tiles, put):
        for n in range(tiles):
            put(n, dot(a, w[:, TILE * n : TILE * n + TILE]))

    def product_t(a, w, tiles, put):
        for n in range(tiles):
            put(n, dot_nt(a, w[TILE * n : TILE * n + TILE, :]))

    def store_to(ref, rows):
        def put(n, value):
            ref[rows, TILE * n : TILE * n + TILE] = value.astype(ref.dtype)
        return put

    def groups_of(first, windows, channels):
        for w in range(first, first + windows):
            for g in range(channels // GROUP):
                yield pl.ds(64 * w, 64), [pl.ds(c * channels + g * GROUP, GROUP) for c in range(3)]

    def attention(qkv, p_ref, out, first, windows, channels, bias_of):
        places = list(groups_of(first, windows, channels))
        items = [tuple(qkv[rows, lanes] for lanes in three) for rows, three in places]
        done = attend(items, [bias[bias_of(rows.start // 64)] for rows, three in places], halves, low)
        for (rows, three), (p, o) in zip(places, done):
            p_ref[rows, three[0]] = p
            out[rows, three[0]] = o.astype(BF16)

    def attention_grad(qkv, p_ref, d_out, first, windows, channels):
        places = list(groups_of(first, windows, channels))
        items = [tuple(qkv[rows, lanes] for lanes in three) for rows, three in places]
        probs = [p_ref[rows, three[0]] for rows, three in places]
        d_outs = [d_out[rows, three[0]] for rows, three in places]
        done = attend_grad(items, probs, d_outs, halves, low)
        for (rows, three), grads in zip(places, done):
            for lanes, value in zip(three, grads):
                qkv[rows, lanes] = value.astype(BF16)

    def window_rows(first, count):
        return slice(64 * first, 64 * (first + count))

    def x_window(w):
        return xs[8 * (w // 8) : 8 * (w // 8) + 8, 8 * (w % 8) : 8 * (w % 8) + 8, :].reshape(64, CH)

    def fine_norm(first, count):
        for w in range(first, first + count):
            (c,), scale = norm_stats([x_window(w)], CH)
            n_f[64 * w : 64 * w + 64, :] = (c * scale * fine_gain[...]).astype(BF16)

    def fine_attend(first, count):
        rows = window_rows(first, count)
        product(n_f[rows, :], w_fq, 3 * CH // TILE, store_to(qkv_f, rows))
        attention(qkv_f, p_f, m_f, first, count, CH, lambda w: w // 8)

    def fine_join(first, count):
        def put(n, value):
            lanes = slice(TILE * n, TILE * n + TILE)
            branch = value.astype(BF16).astype(F32)
            for w in range(first, first + count):
                r, c = 8 * (w // 8), 8 * (w % 8)
                own = branch[64 * (w - first) : 64 * (w - first) + 64]
                full = xs[r : r + 8, c : c + 8, lanes] + own.reshape(8, 8, TILE)
                for j in range(2):
                    fo[4 + r : 12 + r, 2 * n + j, 8 + c : 16 + c, :] = full[:, :, 128 * j : 128 * j + 128]
                if w >= 8:
                    fo_s[0][w - 8, :, lanes] = own[32:].astype(BF16)
                if w % 8 == 7:
                    fo_s[1][32 * (w // 8) : 32 * (w // 8) + 32, lanes] = pieces(own, 4, 4).astype(BF16)
        product(m_f[window_rows(first, count), :], w_fp, CH // TILE, put)

    def spread(ref, row, start, count):
        return jnp.concatenate([ref[row, j, pl.ds(start, count, stride=2), :] for j in range(4)], axis=1)

    def merged(i):
        return [spread(fo, 4 + 2 * i + a, 8 + b, 32) for a in range(2) for b in range(2)]

    for i in range(8):
        xs[i, 0:56, :] = tok[i + 4, 4:60, :]
    fine_norm(0, 7)
    for j in range(4):
        loads["cot%d" % j].wait()
    for i in range(8):
        for j in range(4):
            cot_s[0][i, j] = cotx[i, j, 0:64, :].astype(BF16)
            cot_s[1][i, j] = jnp.concatenate([cotx[2 * i + e, j, 0:8, :] for e in range(2)], axis=0).astype(BF16)
    cot_copies = exchange(3, cot_s, cot_d, (0, 8), (0, 4), True)
    loads["fq"].wait()
    fine_attend(0, 7)
    load("cq", coarse_qkv, w_cq)
    load("cp", coarse_proj, w_cp)
    loads["fp"].wait()
    fine_join(0, 7)
    for c in tok_copies:
        c.wait_recv()
    for i in range(4):
        tok[16 + i, 0:64, :] = tok_d[0][i].astype(F32)
        side = tok_d[1][16 * i : 16 * i + 16, :].astype(F32)
        for e in range(4):
            tok[4 * i + e, 64:68, :] = side[4 * e : 4 * e + 4]
    side = tok_d[2][...].astype(F32)
    for e in range(4):
        tok[16 + e, 64:68, :] = side[4 * e : 4 * e + 4]
    for i in range(8):
        xs[i, 56:64, :] = tok[i + 4, 60:68, :]
        xs[8 + i] = tok[i + 12, 4:68, :]
    fine_norm(7, 9)
    fine_attend(7, 9)
    fine_join(7, 9)
    for i in range(8):
        parts, scale = norm_stats(merged(i), 4 * CH)
        for j, c in enumerate(parts):
            gain = merge_gain[:, CH * j : CH * (j + 1)]
            cells[32 * i : 32 * i + 32, CH * j : CH * (j + 1)] = (c * scale * gain).astype(BF16)
    loads["m"].wait()
    def put_cin(n, value):
        lanes = slice(TILE * n, TILE * n + TILE)
        cin[0:8, 0:32, lanes] = value.reshape(8, 32, TILE)
        cin_s[0][:, :, lanes] = value[0:64].reshape(2, 32, TILE).astype(BF16)
        cin_s[1][:, lanes] = jnp.concatenate([value[32 * i : 32 * i + 2] for i in range(8)], axis=0).astype(BF16)
    product(cells[...], w_m, WIDE // TILE, put_cin)
    cin_copies = exchange(6, cin_s, cin_d, (0, 16), (0, 16), True)
    fo_copies = exchange(9, fo_s, fo_d, (0, 48), (48, 64), False)

    for c in cot_copies:
        c.wait_recv()
    for i in range(8):
        for j in range(4):
            cotx[16 + i, j, 0:64, :] = cot_d[0][i, j].astype(F32)
            side = cot_d[1][i, j].astype(F32)
            for e in range(2):
                cotx[2 * i + e, j, 64:72, :] = side[8 * e : 8 * e + 8]
    for i in range(4):
        for j in range(4):
            side = cot_d[2][i, j].astype(F32)
            for e in range(2):
                cotx[16 + 2 * i + e, j, 64:72, :] = side[8 * e : 8 * e + 8]
    def gather_cot(i, carry):
        for w in range(4):
            for a in range(2):
                for b in range(2):
                    both = [spread(cotx, 8 + 4 * i + 2 * e + a, 8 + 16 * w + b, 8) for e in range(2)]
                    part = 2 * a + b
                    cells[pl.ds(64 * w + 16 * i, 16), CH * part : CH * (part + 1)] = jnp.concatenate(both, axis=0).astype(BF16)
        return carry
    unrolled(0, 4, gather_cot)
    loads["e"].wait()
    everything = slice(0, 256)
    product_t(cells[...], w_e, WIDE // TILE, store_to(dco, everything))

    loads["cp"].wait()
    product_t(dco[...], w_cp, WIDE // TILE, store_to(dm_c, everything))

    for c in cin_copies:
        c.wait_recv()
    for i in range(2):
        cin[8 + i, 0:32, :] = cin_d[0][i].astype(F32)
    side, tip = cin_d[1][...].astype(F32), cin_d[2][...].astype(F32)
    for i in range(2, 8):
        cin[i, 32:34, :] = side[2 * i : 2 * i + 2]
    for i in range(2):
        cin[8 + i, 32:34, :] = tip[2 * i : 2 * i + 2]
    for w in range(4):
        x = cin[2:10, 2 + 8 * w : 10 + 8 * w, :].reshape(64, WIDE)
        xc[64 * w : 64 * w + 64, :] = x
        (c,), scale = norm_stats([x], WIDE)
        n_c[64 * w : 64 * w + 64, :] = (c * scale * coarse_gain[...]).astype(BF16)
    loads["cq"].wait()
    product(n_c[...], w_cq, 3 * WIDE // TILE, store_to(qkv_c, everything))
    attention(qkv_c, p_c, m_c, 0, 4, WIDE, lambda w: 1)
    def put_co(n, value):
        lanes = aligned(n, TILE)
        full = xc[:, lanes] + value.astype(BF16).astype(F32)
        for w in range(4):
            own = full[64 * w : 64 * w + 64]
            co[4:12, 8 + 8 * w : 16 + 8 * w, lanes] = own.reshape(8, 8, TILE)
            co_s[0][w, :, lanes] = own[32:].astype(BF16)
        co_s[1][:, lanes] = pieces(own, 4, 4).astype(BF16)
    product(m_c[...], w_cp, WIDE // TILE, put_co)
    co_copies = exchange(12, co_s, co_d, (0, 16), (16, 32), False)

    attention_grad(qkv_c, p_c, dm_c, 0, 4, WIDE)
    product_t(qkv_c[...], w_cq, WIDE // TILE, store_to(n_c, everything))
    for w in range(4):
        rows = slice(64 * w, 64 * w + 64)
        (d,) = norm_grad([xc[rows, :]], [n_c[rows, :].astype(F32)], [coarse_gain[...]], WIDE)
        full = d + dco[rows, :].astype(F32)
        gci[2:10, 8 + 8 * w : 16 + 8 * w, :] = full.reshape(8, 8, WIDE)
        gci_s[0][w] = full[48:].astype(BF16)
    gci_s[1][...] = pieces(full, 6, 2).astype(BF16)
    gci_copies = exchange(15, gci_s, gci_d, (0, 16), (0, 16), False)

    for c in fo_copies:
        c.wait_recv()
    for w in range(8):
        strip = fo_d[0][w].astype(F32)
        for a in range(4):
            full = tok[a, 4 + 8 * w : 12 + 8 * w, :] + strip[8 * a : 8 * a + 8]
            for j in range(4):
                fo[a, j, 8 + 8 * w : 16 + 8 * w, :] = full[:, 128 * j : 128 * j + 128]
    side, tip = fo_d[1][...].astype(F32), fo_d[2][...].astype(F32)
    for a in range(16):
        full = tok[a, 0:4, :] + (tip[4 * a : 4 * a + 4] if a < 4 else side[4 * a - 16 : 4 * a - 12])
        for j in range(4):
            fo[a, j, 4:8, :] = full[:, 128 * j : 128 * j + 128]
    for c in co_copies:
        c.wait_recv()
    for w in range(4):
        strip = co_d[0][w].astype(F32)
        for a in range(4):
            co[a, 8 + 8 * w : 16 + 8 * w, :] = strip[8 * a : 8 * a + 8]
    side, tip = co_d[1][...].astype(F32), co_d[2][...].astype(F32)
    for a in range(4):
        co[a, 4:8, :] = tip[4 * a : 4 * a + 4]
        co[4 + a, 4:8, :] = side[4 * a : 4 * a + 4]
    for i in range(8):
        n_c[32 * i : 32 * i + 32, :] = co[i, 4:36, :].astype(BF16)
    for a in range(2):
        for b in range(2):
            part = 2 * a + b
            def lift(n, carry):
                w = w_e[:, pl.ds(part * CH + n * TILE, TILE)]
                lifted = dot(n_c[...], w)
                for s in range(2):
                    j = 2 * n + s
                    for i in range(8):
                        part_fo = fo[2 * i + a, j, pl.ds(4 + b, 32, stride=2), :]
                        res[2 * i + a, j, pl.ds(b, 32, stride=2), :] = part_fo + lifted[32 * i : 32 * i + 32, 128 * s : 128 * s + 128]
                return carry
            unrolled(0, CH // TILE, lift)
    out_result = [
        pltpu.make_async_copy(res.at[:, j], result.at[:, :, 128 * j : 128 * j + 128], load_sem.at[12 + j])
        for j in range(4)
    ]
    for c in out_result:
        c.start()

    for c in gci_copies:
        c.wait_recv()
    for w in range(4):
        strip = gci_d[0][w].astype(F32)
        for a in range(2):
            gci[a, 8 + 8 * w : 16 + 8 * w, :] = strip[8 * a : 8 * a + 8]
    side, tip = gci_d[1][...].astype(F32), gci_d[2][...].astype(F32)
    for a in range(6):
        gci[2 + a, 6:8, :] = side[2 * a : 2 * a + 2]
    for a in range(2):
        gci[a, 6:8, :] = tip[12 + 2 * a : 14 + 2 * a]
    for i in range(8):
        n_c[32 * i : 32 * i + 32, :] = gci[i, 6:38, :].astype(BF16)
    product_t(n_c[...], w_m, 4 * CH // TILE, store_to(cells, everything))
    def merge_grad(i, carry):
        gains = [merge_gain[:, CH * j : CH * (j + 1)] for j in range(4)]
        grads = [cells[aligned(i, 32), CH * j : CH * (j + 1)].astype(F32) for j in range(4)]
        done = norm_grad(merged(i), grads, gains, 4 * CH)
        for a in range(2):
            for b in range(2):
                full = spread(cotx, 4 + 2 * i + a, 4 + b, 32) + done[2 * a + b]
                for j in range(4):
                    gf[2 * i + a, j, pl.ds(b, 32, stride=2), :] = full[:, 128 * j : 128 * j + 128]
        return carry
    unrolled(0, 8, merge_grad)

    def window(wr, w):
        return jnp.concatenate(
            [gf[8 * wr : 8 * wr + 8, j, aligned(w, 8), :].reshape(64, 128) for j in range(4)], axis=1)
    gt = tok
    def fine_grad(first, count):
        rows = window_rows(first, count)
        for w in range(first, first + count):
            n_f[64 * w : 64 * w + 64, :] = window(w // 8, w % 8).astype(BF16)
        product_t(n_f[rows, :], w_fp, CH // TILE, store_to(m_f, rows))
        attention_grad(qkv_f, p_f, m_f, first, count, CH)
        product_t(qkv_f[rows, :], w_fq, CH // TILE, store_to(n_f, rows))
        for w in range(first, first + count):
            dn = n_f[64 * w : 64 * w + 64, :].astype(F32)
            (d,) = norm_grad([x_window(w)], [dn], [fine_gain[...]], CH)
            full = window(w // 8, w % 8) + d
            r, c = 8 * (w // 8), 8 * (w % 8)
            gt[4 + r : 12 + r, 8 + c : 16 + c, :] = full.reshape(8, 8, CH)
            if w >= 8:
                gt_s[0][w - 8] = full[32:].astype(BF16)
            if w % 8 == 7:
                gt_s[1][32 * (w // 8) : 32 * (w // 8) + 32, :] = pieces(full, 4, 4).astype(BF16)
    fine_grad(7, 9)
    gt_copies = exchange(18, gt_s, gt_d, (0, 48), (48, 64), False)
    fine_grad(0, 7)
    for c in gt_copies:
        c.wait_recv()
    for w in range(8):
        strip = gt_d[0][w].astype(F32)
        for a in range(4):
            gt[a, 8 + 8 * w : 16 + 8 * w, :] = strip[8 * a : 8 * a + 8]
    side, tip = gt_d[1][...].astype(F32), gt_d[2][...].astype(F32)
    for a in range(16):
        gt[a, 4:8, :] = tip[4 * a : 4 * a + 4] if a < 4 else side[4 * a - 16 : 4 * a - 12]
    for i in range(ROWS):
        xs[i] = gt[i, 4:68, :]
    out_grad = pltpu.make_async_copy(xs, grad, load_sem.at[16])
    out_grad.start()
    for c in tok_copies + cot_copies + cin_copies + fo_copies + co_copies + gci_copies + gt_copies:
        c.wait_send()
    for c in out_result + [out_grad]:
        c.wait()


def exchanged(strip, side, edge, corner):
    vmem = pltpu.VMEM
    return (
        (vmem(strip, BF16), vmem(side, BF16)),
        (vmem(strip, BF16), vmem((edge,) + side[1:], BF16), vmem((corner,) + side[1:], BF16)),
    )


def local(
    tokens, fine_gain, fine_qkv, fine_proj, merge_gain, merge_weight,
    coarse_gain, coarse_qkv, coarse_proj, expand_weight, cotangent,
):
    vmem = pltpu.VMEM
    shape = jax.ShapeDtypeStruct((ROWS, COLS, CH), F32)
    hbm = pl.BlockSpec(memory_space=pl.ANY)
    whole = pl.BlockSpec(memory_space=pltpu.VMEM)
    return pl.pallas_call(
        kernel,
        out_shape=(shape, shape),
        in_specs=[hbm, hbm, whole, whole, whole] + [hbm] * 6,
        out_specs=(hbm, hbm),
        scratch_shapes=[
            vmem((20, 72, CH), F32),
            vmem((24, 4, 72, 128), F32),
            vmem((ROWS, COLS, CH), F32),
            vmem((20, 4, 72, 128), F32),
            vmem((10, 40, WIDE), F32),
            vmem((10, 40, WIDE), F32),
            vmem((12, 40, WIDE), F32),
            vmem((256, WIDE), F32),
            vmem((ROWS, 4, COLS, 128), F32),
            vmem((ROWS, 4, COLS, 128), F32),
            vmem((1024, 3 * CH), BF16),
            vmem((1024, CH), F32),
            vmem((256, 3 * WIDE), BF16),
            vmem((256, WIDE), F32),
            vmem((1024, CH), BF16),
            vmem((1024, CH), BF16),
            vmem((256, 4 * CH), BF16),
            vmem((256, WIDE), BF16),
            vmem((256, WIDE), BF16),
            vmem((256, WIDE), BF16),
            vmem((256, WIDE), BF16),
            vmem((2, 64, GROUP), F32),
            vmem(fine_qkv.shape, BF16),
            vmem(fine_proj.shape, BF16),
            vmem(merge_weight.shape, BF16),
            vmem(coarse_qkv.shape, BF16),
            vmem(coarse_proj.shape, BF16),
            vmem(expand_weight.shape, BF16),
            *exchanged((4, 64, CH), (64, CH), 64, 16),
            *exchanged((8, 4, 64, 128), (8, 4, 16, 128), 8, 4),
            *exchanged((2, 32, WIDE), (16, WIDE), 16, 16),
            *exchanged((8, 32, CH), (64, CH), 48, 16),
            *exchanged((4, 32, WIDE), (32, WIDE), 16, 16),
            *exchanged((4, 16, WIDE), (16, WIDE), 16, 16),
            *exchanged((8, 32, CH), (64, CH), 48, 16),
            pltpu.SemaphoreType.DMA((17,)),
            pltpu.SemaphoreType.DMA((21,)),
            pltpu.SemaphoreType.DMA((21,)),
        ],
        compiler_params=pltpu.CompilerParams(
            collective_id=0, has_side_effects=True, vmem_limit_bytes=63 * 1024 * 1024),
    )(
        tokens, cotangent, fine_gain.reshape(1, -1), merge_gain.reshape(1, -1), coarse_gain.reshape(1, -1),
        fine_qkv, fine_proj, merge_weight, coarse_qkv, coarse_proj, expand_weight,
    )


def solution(mesh):
    field = P("lat", "lon", None)
    placed = (field,) + (P(),) * 9 + (field,)
    return jax.shard_map(local, mesh=mesh, in_specs=placed, out_specs=(field, field), check_vma=False)
```

```python
import functools
import math

import jax
import jax.numpy as jnp
from jax import lax
from jax.experimental import pallas as pl
from jax.experimental.pallas import tpu as pltpu
from jax.sharding import PartitionSpec as P

F32 = jnp.float32
BF16 = jnp.bfloat16
MESH = pl.DeviceIdType.MESH

ROWS, COLS, CH = 16, 64, 512
CROWS, CCOLS, WIDE = 8, 32, 1024
HEAD = 64
GROUP = 256
TILE = 256
EXP_SCALE = math.log2(math.e) / math.sqrt(HEAD)


def dot(a, b):
    return jnp.dot(a, b, preferred_element_type=F32)


def dot_nt(a, b):
    return lax.dot_general(a, b, (((1,), (1,)), ((), ())), preferred_element_type=F32)


def dot_tn(a, b):
    return lax.dot_general(a, b, (((0,), (0,)), ((), ())), preferred_element_type=F32)


def norm_stats(parts, width):
    mean = sum(jnp.sum(p, axis=-1, keepdims=True) for p in parts) * (1.0 / width)
    centred = [p - mean for p in parts]
    spread = sum(jnp.sum(c * c, axis=-1, keepdims=True) for c in centred) * (1.0 / width)
    return centred, lax.rsqrt(spread + 1e-05)


def norm_grad(parts, grads, gains, width):
    centred, scale = norm_stats(parts, width)
    xhat = [c * scale for c in centred]
    gy = [d * g for d, g in zip(grads, gains)]
    first = sum(jnp.sum(y, axis=-1, keepdims=True) for y in gy) * (1.0 / width)
    second = sum(jnp.sum(y * x, axis=-1, keepdims=True) for y, x in zip(gy, xhat)) * (1.0 / width)
    return [scale * (y - first - x * second) for y, x in zip(gy, xhat)]


def block_diagonal(x, halves):
    zero = jnp.zeros((64, 128), BF16)
    rows = []
    for h in range(4):
        piece = x[:, 128 * (h // 2) : 128 * (h // 2) + 128] * halves[h % 2]
        rows.append(jnp.concatenate([piece, zero] if h < 2 else [zero, piece], axis=1))
    return jnp.concatenate(rows, axis=0)


def per_query(weights, values, low):
    out = []
    for t in range(2):
        lanes = slice(128 * t, 128 * t + 128)
        full = dot_tn(weights[:, lanes], values[:, lanes])
        out.append(jnp.where(low, full[:64], full[64:]))
    return jnp.concatenate(out, axis=1)


def attend(items, biases, halves, low):
    scores = [dot_nt(k, block_diagonal(q, halves)) + b for (q, k, v), b in zip(items, biases)]
    probs = []
    for s in scores:
        e = jnp.exp2((s - jnp.max(s, axis=0, keepdims=True)) * EXP_SCALE)
        probs.append(e * (1.0 / jnp.sum(e, axis=0, keepdims=True)))
    return [(p, per_query(p.astype(BF16), v, low)) for p, (q, k, v) in zip(probs, items)]


def attend_grad(items, probs, d_outs, halves, low):
    d_diags = [block_diagonal(d, halves) for d in d_outs]
    dps = [dot_nt(v, d) for (q, k, v), d in zip(items, d_diags)]
    dvs = [dot(p.astype(BF16), d) for p, d in zip(probs, d_diags)]
    dss = []
    for p, dp in zip(probs, dps):
        weighted = p * dp
        dss.append(((weighted - p * jnp.sum(weighted, axis=0, keepdims=True)) * (1.0 / math.sqrt(HEAD))).astype(BF16))
    dks = [dot(ds, block_diagonal(q, halves)) for ds, (q, k, v) in zip(dss, items)]
    dqs = [per_query(ds, k, low) for ds, (q, k, v) in zip(dss, items)]
    return list(zip(dqs, dks, dvs))


def aligned(i, step):
    return pl.ds(i * step, step)


def unrolled(first, last, step):
    for i in range(first, last):
        step(i, 0)


def kernel(
    tokens, cot, fine_gain, merge_gain, coarse_gain,
    fine_qkv, fine_proj, merge_w, coarse_qkv, coarse_proj, expand_w,
    result, grad,
    tok, cotx, xs, fo, cin, gci, co, xc, gf, res,
    qkv_f, p_f, qkv_c, p_c, n_f, m_f, cells, n_c, m_c, dm_c, dco, bias,
    w_fq, w_fp, w_m, w_cq, w_cp, w_e,
    tok_s, tok_d, cot_s, cot_d, dco_s, dco_d, cin_s, cin_d, fo_s, fo_d, co_s, co_d, gci_s, gci_d, gt_s, gt_d,
    load_sem, send_sem, recv_sem,
):
    lat, lon = lax.axis_index("lat"), lax.axis_index("lon")
    n_lat, n_lon = lax.axis_size("lat"), lax.axis_size("lon")
    up, down = lax.rem(lat + n_lat - 1, n_lat), lax.rem(lat + 1, n_lat)
    west, east = lax.rem(lon + n_lon - 1, n_lon), lax.rem(lon + 1, n_lon)

    barrier = pltpu.get_barrier_semaphore()
    for a, o in ((up, lon), (lat, west), (up, west), (down, lon), (lat, east), (down, east)):
        pl.semaphore_signal(barrier, inc=1, device_id={"lat": a, "lon": o}, device_id_type=MESH)

    loads = {}
    def load(name, src, dst):
        loads[name] = pltpu.make_async_copy(src, dst, load_sem.at[len(loads)])
        loads[name].start()

    load("top", tokens.at[0:4], tok.at[0:4, 0:COLS])
    load("side", tokens.at[4:ROWS, 0:8], tok.at[4:ROWS, 0:8])
    load("tok", tokens.at[4:ROWS, 8:COLS], tok.at[4:ROWS, 8:COLS])
    load("fq", fine_qkv, w_fq)
    for j in range(4):
        load("cot%d" % j, cot.at[:, :, 128 * j : 128 * j + 128], cotx.at[0:ROWS, j, 0:COLS])

    def exchange(first, sent, landed, edge, corner, ahead):
        targets = ((up, lon), (lat, west), (up, west)) if ahead else ((down, lon), (lat, east), (down, east))
        sources = (sent[0], sent[1].at[edge[0] : edge[1]], sent[1].at[corner[0] : corner[1]])
        copies = []
        for i, (src, dst, (a, o)) in enumerate(zip(sources, landed, targets)):
            copies.append(pltpu.make_async_remote_copy(
                src_ref=src, dst_ref=dst, send_sem=send_sem.at[first + i], recv_sem=recv_sem.at[first + i],
                device_id={"lat": a, "lon": o}, device_id_type=MESH))
            copies[-1].start()
        return copies

    def pieces(value, start, size):
        return jnp.concatenate([value[8 * a + start : 8 * a + start + size] for a in range(value.shape[0] // 8)], axis=0)

    loads["top"].wait()
    loads["side"].wait()
    for i in range(4):
        tok_s[0][i] = tok[i, 0:64, :].astype(BF16)
        tok_s[1][16 * i : 16 * i + 16, :] = jnp.concatenate([tok[4 * i + e, 0:4, :] for e in range(4)], axis=0).astype(BF16)
    pl.semaphore_wait(barrier, 6)
    tok_copies = exchange(0, tok_s, tok_d, (16, 64), (0, 16), True)
    loads["tok"].wait()
    load("fp", fine_proj, w_fp)
    load("e", expand_w, w_e)
    load("m", merge_w, w_m)

    lane = lax.broadcasted_iota(jnp.int32, (1, 128), 1)
    low = lane < 64
    halves = [low.astype(F32).astype(BF16), (lane >= 64).astype(F32).astype(BF16)]
    keys = lax.broadcasted_iota(jnp.int32, (64, GROUP), 0) // 32
    queries = (lax.broadcasted_iota(jnp.int32, (64, GROUP), 1) // 32) % 2
    last = jnp.where(lat == n_lat - 1, 1, 0)
    bias[0] = jnp.zeros((64, GROUP), F32)
    bias[1] = jnp.where((keys != queries) & (last == 1), -jnp.inf, 0.0)

    def product(a, w, tiles, put):
        for n in range(tiles):
            put(n, dot(a, w[:, TILE * n : TILE * n + TILE]))

    def product_t(a, w, tiles, put):
        for n in range(tiles):
            put(n, dot_nt(a, w[TILE * n : TILE * n + TILE, :]))

    def store_to(ref, rows):
        def put(n, value):
            ref[rows, TILE * n : TILE * n + TILE] = value.astype(ref.dtype)
        return put

    def groups_of(first, windows, channels):
        for w in range(first, first + windows):
            for g in range(channels // GROUP):
                yield pl.ds(64 * w, 64), [pl.ds(c * channels + g * GROUP, GROUP) for c in range(3)]

    def attention(qkv, p_ref, out, first, windows, channels, bias_of):
        places = list(groups_of(first, windows, channels))
        items = [tuple(qkv[rows, lanes] for lanes in three) for rows, three in places]
        done = attend(items, [bias[bias_of(rows.start // 64)] for rows, three in places], halves, low)
        for (rows, three), (p, o) in zip(places, done):
            p_ref[rows, three[0]] = p
            out[rows, three[0]] = o.astype(BF16)

    def attention_grad(qkv, p_ref, d_out, first, windows, channels):
        places = list(groups_of(first, windows, channels))
        items = [tuple(qkv[rows, lanes] for lanes in three) for rows, three in places]
        probs = [p_ref[rows, three[0]] for rows, three in places]
        d_outs = [d_out[rows, three[0]] for rows, three in places]
        done = attend_grad(items, probs, d_outs, halves, low)
        for (rows, three), grads in zip(places, done):
            for lanes, value in zip(three, grads):
                qkv[rows, lanes] = value.astype(BF16)

    def window_rows(first, count):
        return slice(64 * first, 64 * (first + count))

    def x_window(w):
        return xs[8 * (w // 8) : 8 * (w // 8) + 8, 8 * (w % 8) : 8 * (w % 8) + 8, :].reshape(64, CH)

    def fine_norm(first, count):
        for w in range(first, first + count):
            (c,), scale = norm_stats([x_window(w)], CH)
            n_f[64 * w : 64 * w + 64, :] = (c * scale * fine_gain[...]).astype(BF16)

    def fine_attend(first, count):
        rows = window_rows(first, count)
        product(n_f[rows, :], w_fq, 3 * CH // TILE, store_to(qkv_f, rows))
        attention(qkv_f, p_f, m_f, first, count, CH, lambda w: w // 8)

    def fine_join(first, count):
        def put(n, value):
            lanes = slice(TILE * n, TILE * n + TILE)
            branch = value.astype(BF16).astype(F32)
            for w in range(first, first + count):
                r, c = 8 * (w // 8), 8 * (w % 8)
                own = branch[64 * (w - first) : 64 * (w - first) + 64]
                full = xs[r : r + 8, c : c + 8, lanes] + own.reshape(8, 8, TILE)
                for j in range(2):
                    fo[4 + r : 12 + r, 2 * n + j, 8 + c : 16 + c, :] = full[:, :, 128 * j : 128 * j + 128]
                if w >= 8:
                    fo_s[0][w - 8, :, lanes] = own[32:].astype(BF16)
                if w % 8 == 7:
                    fo_s[1][32 * (w // 8) : 32 * (w // 8) + 32, lanes] = pieces(own, 4, 4).astype(BF16)
        product(m_f[window_rows(first, count), :], w_fp, CH // TILE, put)

    def spread(ref, row, start, count):
        return jnp.concatenate([ref[row, j, pl.ds(start, count, stride=2), :] for j in range(4)], axis=1)

    def merged(row, col, count):
        return [spread(fo, 4 + 2 * row + a, 8 + 2 * col + b, count) for a in range(2) for b in range(2)]

    batch_a = [(i, 0, 32, 32 * i) for i in range(4)] + [(4 + i, 0, 16, 128 + 16 * i) for i in range(4)]
    batch_b = [(4 + i, 16, 16, 192 + 16 * i) for i in range(4)]

    for i in range(8):
        xs[i, 0:56, :] = tok[i + 4, 4:60, :]
    fine_norm(0, 7)
    for j in range(4):
        loads["cot%d" % j].wait()
    for i in range(4):
        for j in range(4):
            cot_s[0][i, j] = cotx[i, j, 0:64, :].astype(BF16)
            cot_s[1][i, j] = jnp.concatenate([cotx[4 * i + e, j, 0:4, :] for e in range(4)], axis=0).astype(BF16)
    cot_copies = exchange(3, cot_s, cot_d, (1, 4), (0, 1), True)
    loads["fq"].wait()
    fine_attend(0, 7)
    load("cq", coarse_qkv, w_cq)
    load("cp", coarse_proj, w_cp)
    loads["fp"].wait()
    fine_join(0, 7)
    for i in range(8):
        for a in range(2):
            for b in range(2):
                part = 2 * a + b
                cells[32 * i : 32 * i + 32, CH * part : CH * (part + 1)] = spread(cotx, 2 * i + a, b, 32).astype(BF16)
    loads["e"].wait()
    everything = slice(0, 256)
    def put_dco(n, value):
        lanes = slice(TILE * n, TILE * n + TILE)
        dco_s[0][:, :, lanes] = value[0:128].reshape(4, 32, TILE).astype(BF16)
        dco_s[1][:, lanes] = jnp.concatenate([value[32 * i : 32 * i + 4] for i in range(8)], axis=0).astype(BF16)
        co[0:4, 0:32, lanes] = value[128:256].reshape(4, 32, TILE)
    product_t(cells[...], w_e, WIDE // TILE, put_dco)
    dco_copies = exchange(21, dco_s, dco_d, (16, 32), (0, 16), True)
    for c in tok_copies:
        c.wait_recv()
    for i in range(4):
        tok[16 + i, 0:64, :] = tok_d[0][i].astype(F32)
    for i in range(1, 4):
        side = tok_d[1][16 * i - 16 : 16 * i, :].astype(F32)
        for e in range(4):
            tok[4 * i + e, 64:68, :] = side[4 * e : 4 * e + 4]
    side = tok_d[2][...].astype(F32)
    for e in range(4):
        tok[16 + e, 64:68, :] = side[4 * e : 4 * e + 4]
    for i in range(8):
        xs[i, 56:64, :] = tok[i + 4, 60:68, :]
        xs[8 + i] = tok[i + 12, 4:68, :]
    fine_norm(7, 5)
    fine_attend(7, 5)
    fine_join(7, 5)
    def merge_norm(batch):
        for row, col, count, at in batch:
            parts, scale = norm_stats(merged(row, col, count), 4 * CH)
            for j, c in enumerate(parts):
                gain = merge_gain[:, CH * j : CH * (j + 1)]
                cells[at : at + count, CH * j : CH * (j + 1)] = (c * scale * gain).astype(BF16)
    merge_norm(batch_a)
    loads["m"].wait()
    def put_cin(n, value):
        lanes = slice(TILE * n, TILE * n + TILE)
        cin[0:4, 0:32, lanes] = value[0:128].reshape(4, 32, TILE)
        cin[4:8, 0:16, lanes] = value[128:192].reshape(4, 16, TILE)
        cin_s[0][:, :, lanes] = value[0:64].reshape(2, 32, TILE).astype(BF16)
        starts = [32 * i for i in range(4)] + [128 + 16 * i for i in range(4)]
        cin_s[1][:, lanes] = jnp.concatenate([value[i : i + 2] for i in starts], axis=0).astype(BF16)
    product(cells[0:192, :], w_m, WIDE // TILE, put_cin)
    cin_copies = exchange(6, cin_s, cin_d, (0, 16), (0, 16), True)
    fine_norm(12, 4)
    fine_attend(12, 4)
    fine_join(12, 4)
    merge_norm(batch_b)
    def put_cin_b(n, value):
        cin[4:8, 16:32, TILE * n : TILE * n + TILE] = value.reshape(4, 16, TILE)
    product(cells[192:256, :], w_m, WIDE // TILE, put_cin_b)

    for c in dco_copies:
        c.wait_recv()
    for i in range(4):
        co[4 + i, 0:32, :] = dco_d[0][i].astype(F32)
    side, tip = dco_d[1][...].astype(F32), dco_d[2][...].astype(F32)
    for i in range(4):
        co[i, 32:36, :] = side[4 * i : 4 * i + 4]
        co[4 + i, 32:36, :] = tip[4 * i : 4 * i + 4]
    for w in range(4):
        dco[64 * w : 64 * w + 64, :] = co[0:8, 4 + 8 * w : 12 + 8 * w, :].reshape(64, WIDE).astype(BF16)
    loads["cp"].wait()
    product_t(dco[...], w_cp, WIDE // TILE, store_to(dm_c, everything))

    for c in cin_copies:
        c.wait_recv()
    fo_copies = exchange(9, fo_s, fo_d, (0, 48), (48, 64), False)
    for i in range(2):
        cin[8 + i, 0:32, :] = cin_d[0][i].astype(F32)
    side, tip = cin_d[1][...].astype(F32), cin_d[2][...].astype(F32)
    for i in range(2, 8):
        cin[i, 32:34, :] = side[2 * i : 2 * i + 2]
    for i in range(2):
        cin[8 + i, 32:34, :] = tip[2 * i : 2 * i + 2]
    for w in range(4):
        x = cin[2:10, 2 + 8 * w : 10 + 8 * w, :].reshape(64, WIDE)
        xc[64 * w : 64 * w + 64, :] = x
        (c,), scale = norm_stats([x], WIDE)
        n_c[64 * w : 64 * w + 64, :] = (c * scale * coarse_gain[...]).astype(BF16)
    loads["cq"].wait()
    product(n_c[...], w_cq, 3 * WIDE // TILE, store_to(qkv_c, everything))
    attention(qkv_c, p_c, m_c, 0, 4, WIDE, lambda w: 1)
    def put_co(n, value):
        lanes = aligned(n, TILE)
        full = xc[:, lanes] + value.astype(BF16).astype(F32)
        for w in range(4):
            own = full[64 * w : 64 * w + 64]
            co[4:12, 8 + 8 * w : 16 + 8 * w, lanes] = own.reshape(8, 8, TILE)
            co_s[0][w, :, lanes] = own[32:].astype(BF16)
        co_s[1][:, lanes] = pieces(own, 4, 4).astype(BF16)
    product(m_c[...], w_cp, WIDE // TILE, put_co)
    co_copies = exchange(12, co_s, co_d, (0, 16), (16, 32), False)

    attention_grad(qkv_c, p_c, dm_c, 0, 4, WIDE)
    product_t(qkv_c[...], w_cq, WIDE // TILE, store_to(n_c, everything))
    for w in range(4):
        rows = slice(64 * w, 64 * w + 64)
        (d,) = norm_grad([xc[rows, :]], [n_c[rows, :].astype(F32)], [coarse_gain[...]], WIDE)
        full = d + dco[rows, :].astype(F32)
        gci[2:10, 8 + 8 * w : 16 + 8 * w, :] = full.reshape(8, 8, WIDE)
        gci_s[0][w] = full[48:].astype(BF16)
    gci_s[1][...] = pieces(full, 6, 2).astype(BF16)
    gci_copies = exchange(15, gci_s, gci_d, (0, 16), (0, 16), False)

    def merge_grad(batch):
        first, last = batch[0][3], batch[-1][3] + batch[-1][2]
        for row, col, count, at in batch:
            n_c[at : at + count, :] = gci[row, 6 + col : 6 + col + count, :].astype(BF16)
        product_t(n_c[first:last, :], w_m, 4 * CH // TILE, store_to(cells, slice(first, last)))
        gains = [merge_gain[:, CH * j : CH * (j + 1)] for j in range(4)]
        for row, col, count, at in batch:
            grads = [cells[at : at + count, CH * j : CH * (j + 1)].astype(F32) for j in range(4)]
            done = norm_grad(merged(row, col, count), grads, gains, 4 * CH)
            for a in range(2):
                for b in range(2):
                    full = spread(cotx, 4 + 2 * row + a, 4 + 2 * col + b, count) + done[2 * a + b]
                    for j in range(4):
                        gf[2 * row + a, j, pl.ds(2 * col + b, count, stride=2), :] = full[:, 128 * j : 128 * j + 128]

    def window(wr, w):
        return jnp.concatenate(
            [gf[8 * wr : 8 * wr + 8, j, aligned(w, 8), :].reshape(64, 128) for j in range(4)], axis=1)
    gt = tok
    def fine_grad(first, count):
        rows = window_rows(first, count)
        for w in range(first, first + count):
            n_f[64 * w : 64 * w + 64, :] = window(w // 8, w % 8).astype(BF16)
        product_t(n_f[rows, :], w_fp, CH // TILE, store_to(m_f, rows))
        attention_grad(qkv_f, p_f, m_f, first, count, CH)
        product_t(qkv_f[rows, :], w_fq, CH // TILE, store_to(n_f, rows))
        for w in range(first, first + count):
            dn = n_f[64 * w : 64 * w + 64, :].astype(F32)
            (d,) = norm_grad([x_window(w)], [dn], [fine_gain[...]], CH)
            full = window(w // 8, w % 8) + d
            r, c = 8 * (w // 8), 8 * (w % 8)
            gt[4 + r : 12 + r, 8 + c : 16 + c, :] = full.reshape(8, 8, CH)
            if w >= 8:
                gt_s[0][w - 8] = full[32:].astype(BF16)
            if w % 8 == 7:
                gt_s[1][32 * (w // 8) : 32 * (w // 8) + 32, :] = pieces(full, 4, 4).astype(BF16)
    for c in cot_copies:
        c.wait_recv()
    for i in range(4):
        for j in range(4):
            cotx[16 + i, j, 0:64, :] = cot_d[0][i, j].astype(F32)
    for i in range(1, 5):
        for j in range(4):
            side = (cot_d[1][i - 1, j] if i < 4 else cot_d[2][0, j]).astype(F32)
            for e in range(4):
                cotx[4 * i + e, j, 64:68, :] = side[4 * e : 4 * e + 4]
    merge_grad(batch_b)
    fine_grad(12, 4)
    gt_first = pltpu.make_async_remote_copy(
        src_ref=gt_s[0].at[4:8], dst_ref=gt_d[0].at[4:8], send_sem=send_sem.at[24], recv_sem=recv_sem.at[24],
        device_id={"lat": down, "lon": lon}, device_id_type=MESH)
    gt_first.start()
    for c in fo_copies:
        c.wait_recv()
    for w in range(8):
        strip = fo_d[0][w].astype(F32)
        for a in range(4):
            full = tok[a, 4 + 8 * w : 12 + 8 * w, :] + strip[8 * a : 8 * a + 8]
            for j in range(4):
                fo[a, j, 8 + 8 * w : 16 + 8 * w, :] = full[:, 128 * j : 128 * j + 128]
    side, tip = fo_d[1][...].astype(F32), fo_d[2][...].astype(F32)
    for a in range(16):
        full = tok[a, 0:4, :] + (tip[4 * a : 4 * a + 4] if a < 4 else side[4 * a - 16 : 4 * a - 12])
        for j in range(4):
            fo[a, j, 4:8, :] = full[:, 128 * j : 128 * j + 128]
    for c in co_copies:
        c.wait_recv()
    for w in range(4):
        strip = co_d[0][w].astype(F32)
        for a in range(4):
            co[a, 8 + 8 * w : 16 + 8 * w, :] = strip[8 * a : 8 * a + 8]
    side, tip = co_d[1][...].astype(F32), co_d[2][...].astype(F32)
    for a in range(4):
        co[a, 4:8, :] = tip[4 * a : 4 * a + 4]
        co[4 + a, 4:8, :] = side[4 * a : 4 * a + 4]
    for i in range(8):
        n_c[32 * i : 32 * i + 32, :] = co[i, 4:36, :].astype(BF16)
    for a in range(2):
        for b in range(2):
            part = 2 * a + b
            def lift(n, carry):
                w = w_e[:, pl.ds(part * CH + n * TILE, TILE)]
                lifted = dot(n_c[...], w)
                for s in range(2):
                    j = 2 * n + s
                    for i in range(8):
                        part_fo = fo[2 * i + a, j, pl.ds(4 + b, 32, stride=2), :]
                        res[2 * i + a, j, pl.ds(b, 32, stride=2), :] = part_fo + lifted[32 * i : 32 * i + 32, 128 * s : 128 * s + 128]
                return carry
            unrolled(0, CH // TILE, lift)
    out_result = [
        pltpu.make_async_copy(res.at[:, j], result.at[:, :, 128 * j : 128 * j + 128], load_sem.at[14 + j])
        for j in range(4)
    ]
    for c in out_result:
        c.start()

    for c in gci_copies:
        c.wait_recv()
    for w in range(4):
        strip = gci_d[0][w].astype(F32)
        for a in range(2):
            gci[a, 8 + 8 * w : 16 + 8 * w, :] = strip[8 * a : 8 * a + 8]
    side, tip = gci_d[1][...].astype(F32), gci_d[2][...].astype(F32)
    for a in range(6):
        gci[2 + a, 6:8, :] = side[2 * a : 2 * a + 2]
    for a in range(2):
        gci[a, 6:8, :] = tip[12 + 2 * a : 14 + 2 * a]
    merge_grad(batch_a)
    fine_grad(7, 5)
    gt_copies = exchange(
        18, (gt_s[0].at[0:4], gt_s[1]), (gt_d[0].at[0:4], gt_d[1], gt_d[2]), (0, 48), (48, 64), False)
    fine_grad(0, 7)
    gt_copies.append(gt_first)
    for c in gt_copies:
        c.wait_recv()
    for w in range(8):
        strip = gt_d[0][w].astype(F32)
        for a in range(4):
            gt[a, 8 + 8 * w : 16 + 8 * w, :] = strip[8 * a : 8 * a + 8]
    side, tip = gt_d[1][...].astype(F32), gt_d[2][...].astype(F32)
    for a in range(16):
        gt[a, 4:8, :] = tip[4 * a : 4 * a + 4] if a < 4 else side[4 * a - 16 : 4 * a - 12]
    for i in range(ROWS):
        xs[i] = gt[i, 4:68, :]
    out_grad = pltpu.make_async_copy(xs, grad, load_sem.at[13])
    out_grad.start()
    for c in tok_copies + cot_copies + dco_copies + cin_copies + fo_copies + co_copies + gci_copies + gt_copies:
        c.wait_send()
    for c in out_result + [out_grad]:
        c.wait()


def exchanged(strip, side, edge, corner):
    vmem = pltpu.VMEM
    return (
        (vmem(strip, BF16), vmem(side, BF16)),
        (vmem(strip, BF16), vmem((edge,) + side[1:], BF16), vmem((corner,) + side[1:], BF16)),
    )


def local(
    tokens, fine_gain, fine_qkv, fine_proj, merge_gain, merge_weight,
    coarse_gain, coarse_qkv, coarse_proj, expand_weight, cotangent,
):
    vmem = pltpu.VMEM
    shape = jax.ShapeDtypeStruct((ROWS, COLS, CH), F32)
    hbm = pl.BlockSpec(memory_space=pl.ANY)
    whole = pl.BlockSpec(memory_space=pltpu.VMEM)
    done = pl.pallas_call(
        kernel,
        out_shape=(shape, shape),
        in_specs=[hbm, hbm, whole, whole, whole] + [hbm] * 6,
        out_specs=(hbm, hbm),
        scratch_shapes=[
            vmem((20, 72, CH), F32),
            vmem((20, 4, 72, 128), F32),
            vmem((ROWS, COLS, CH), F32),
            vmem((20, 4, 72, 128), F32),
            vmem((10, 40, WIDE), F32),
            vmem((10, 40, WIDE), F32),
            vmem((12, 40, WIDE), F32),
            vmem((256, WIDE), F32),
            vmem((ROWS, 4, COLS, 128), F32),
            vmem((ROWS, 4, COLS, 128), F32),
            vmem((1024, 3 * CH), BF16),
            vmem((1024, CH), F32),
            vmem((256, 3 * WIDE), BF16),
            vmem((256, WIDE), F32),
            vmem((1024, CH), BF16),
            vmem((1024, CH), BF16),
            vmem((256, 4 * CH), BF16),
            vmem((256, WIDE), BF16),
            vmem((256, WIDE), BF16),
            vmem((256, WIDE), BF16),
            vmem((256, WIDE), BF16),
            vmem((2, 64, GROUP), F32),
            vmem(fine_qkv.shape, BF16),
            vmem(fine_proj.shape, BF16),
            vmem(merge_weight.shape, BF16),
            vmem(coarse_qkv.shape, BF16),
            vmem(coarse_proj.shape, BF16),
            vmem(expand_weight.shape, BF16),
            *exchanged((4, 64, CH), (64, CH), 48, 16),
            *exchanged((4, 4, 64, 128), (4, 4, 16, 128), 3, 1),
            *exchanged((4, 32, WIDE), (32, WIDE), 16, 16),
            *exchanged((2, 32, WIDE), (16, WIDE), 16, 16),
            *exchanged((8, 32, CH), (64, CH), 48, 16),
            *exchanged((4, 32, WIDE), (32, WIDE), 16, 16),
            *exchanged((4, 16, WIDE), (16, WIDE), 16, 16),
            *exchanged((8, 32, CH), (64, CH), 48, 16),
            pltpu.SemaphoreType.DMA((18,)),
            pltpu.SemaphoreType.DMA((25,)),
            pltpu.SemaphoreType.DMA((25,)),
        ],
        compiler_params=pltpu.CompilerParams(
            collective_id=0, has_side_effects=True, vmem_limit_bytes=63 * 1024 * 1024),
    )(
        tokens, cotangent, fine_gain.reshape(1, -1), merge_gain.reshape(1, -1), coarse_gain.reshape(1, -1),
        fine_qkv, fine_proj, merge_weight, coarse_qkv, coarse_proj, expand_weight,
    )
    return pl.pallas_call(
        hand_over,
        out_shape=(shape, shape),
        in_specs=[hbm, hbm],
        out_specs=(hbm, hbm),
        scratch_shapes=[
            pltpu.VMEM((8, 4, COLS, CH), F32), pltpu.SemaphoreType.DMA((8,)), pltpu.SemaphoreType.DMA((8,))],
    )(*done)


def hand_over(result, grad, result_out, grad_out, held, load_sem, store_sem):
    loads, stores = [], []
    for i, (src, dst) in enumerate(((result, result_out), (grad, grad_out))):
        for part in range(4):
            rows, slot = pl.ds(4 * part, 4), 4 * i + part
            loads.append(pltpu.make_async_copy(src.at[rows], held.at[slot], load_sem.at[slot]))
            stores.append(pltpu.make_async_copy(held.at[slot], dst.at[rows], store_sem.at[slot]))
            loads[-1].start()
    for load, store in zip(loads, stores):
        load.wait()
        store.start()
    for store in stores:
        store.wait()


def solution(mesh):
    field = P("lat", "lon", None)
    placed = (field,) + (P(),) * 9 + (field,)
    return jax.shard_map(local, mesh=mesh, in_specs=placed, out_specs=(field, field), check_vma=False)
```

```python
import functools
import math

import jax
import jax.numpy as jnp
from jax import lax
from jax.experimental import pallas as pl
from jax.experimental.pallas import tpu as pltpu
from jax.sharding import PartitionSpec as P

F32 = jnp.float32
BF16 = jnp.bfloat16
MESH = pl.DeviceIdType.MESH

ROWS, COLS, CH = 16, 64, 512
CROWS, CCOLS, WIDE = 8, 32, 1024
HEAD = 64
GROUP = 256
TILE = 256
EXP_SCALE = math.log2(math.e) / math.sqrt(HEAD)


def dot(a, b):
    return jnp.dot(a, b, preferred_element_type=F32)


def dot_nt(a, b):
    return lax.dot_general(a, b, (((1,), (1,)), ((), ())), preferred_element_type=F32)


def dot_tn(a, b):
    return lax.dot_general(a, b, (((0,), (0,)), ((), ())), preferred_element_type=F32)


def norm_stats(parts, width):
    mean = sum(jnp.sum(p, axis=-1, keepdims=True) for p in parts) * (1.0 / width)
    centred = [p - mean for p in parts]
    spread = sum(jnp.sum(c * c, axis=-1, keepdims=True) for c in centred) * (1.0 / width)
    return centred, lax.rsqrt(spread + 1e-05)


def norm_grad(parts, grads, gains, width):
    centred, scale = norm_stats(parts, width)
    xhat = [c * scale for c in centred]
    gy = [d * g for d, g in zip(grads, gains)]
    first = sum(jnp.sum(y, axis=-1, keepdims=True) for y in gy) * (1.0 / width)
    second = sum(jnp.sum(y * x, axis=-1, keepdims=True) for y, x in zip(gy, xhat)) * (1.0 / width)
    return [scale * (y - first - x * second) for y, x in zip(gy, xhat)]


def block_diagonal(x, halves):
    zero = jnp.zeros((64, 128), BF16)
    rows = []
    for h in range(4):
        piece = x[:, 128 * (h // 2) : 128 * (h // 2) + 128] * halves[h % 2]
        rows.append(jnp.concatenate([piece, zero] if h < 2 else [zero, piece], axis=1))
    return jnp.concatenate(rows, axis=0)


def per_query(weights, values, low):
    out = []
    for t in range(2):
        lanes = slice(128 * t, 128 * t + 128)
        full = dot_tn(weights[:, lanes], values[:, lanes])
        out.append(jnp.where(low, full[:64], full[64:]))
    return jnp.concatenate(out, axis=1)


def attend(items, biases, halves, low):
    scores = [dot_nt(k, block_diagonal(q, halves)) + b for (q, k, v), b in zip(items, biases)]
    probs = []
    for s in scores:
        e = jnp.exp2((s - jnp.max(s, axis=0, keepdims=True)) * EXP_SCALE)
        probs.append(e * (1.0 / jnp.sum(e, axis=0, keepdims=True)))
    return [(p, per_query(p.astype(BF16), v, low)) for p, (q, k, v) in zip(probs, items)]


def attend_grad(items, probs, d_outs, halves, low):
    d_diags = [block_diagonal(d, halves) for d in d_outs]
    dps = [dot_nt(v, d) for (q, k, v), d in zip(items, d_diags)]
    dvs = [dot(p.astype(BF16), d) for p, d in zip(probs, d_diags)]
    dss = []
    for p, dp in zip(probs, dps):
        weighted = p * dp
        dss.append(((weighted - p * jnp.sum(weighted, axis=0, keepdims=True)) * (1.0 / math.sqrt(HEAD))).astype(BF16))
    dks = [dot(ds, block_diagonal(q, halves)) for ds, (q, k, v) in zip(dss, items)]
    dqs = [per_query(ds, k, low) for ds, (q, k, v) in zip(dss, items)]
    return list(zip(dqs, dks, dvs))


def aligned(i, step):
    return pl.ds(i * step, step)


def unrolled(first, last, step):
    for i in range(first, last):
        step(i, 0)


def kernel(
    tokens, cot, fine_gain, merge_gain, coarse_gain,
    fine_qkv, fine_proj, merge_w, coarse_qkv, coarse_proj, expand_w,
    result, grad,
    tok, cotx, xs, fo, cin, gci, co, xc, gf, res,
    qkv_f, p_f, qkv_c, p_c, n_f, m_f, cells, n_c, m_c, dm_c, dco, bias,
    w_fq, w_fp, w_m, w_cq, w_cp, w_e,
    tok_s, tok_d, cot_s, cot_d, dco_s, dco_d, cin_s, cin_d, fo_s, fo_d, co_s, co_d, gci_s, gci_d, gt_s, gt_d,
    load_sem, send_sem, recv_sem,
):
    lat, lon = lax.axis_index("lat"), lax.axis_index("lon")
    n_lat, n_lon = lax.axis_size("lat"), lax.axis_size("lon")
    up, down = lax.rem(lat + n_lat - 1, n_lat), lax.rem(lat + 1, n_lat)
    west, east = lax.rem(lon + n_lon - 1, n_lon), lax.rem(lon + 1, n_lon)

    barrier = pltpu.get_barrier_semaphore()
    for a, o in ((up, lon), (lat, west), (up, west), (down, lon), (lat, east), (down, east)):
        pl.semaphore_signal(barrier, inc=1, device_id={"lat": a, "lon": o}, device_id_type=MESH)

    loads = {}
    def load(name, src, dst):
        loads[name] = pltpu.make_async_copy(src, dst, load_sem.at[len(loads)])
        loads[name].start()

    load("top", tokens.at[0:4], tok.at[0:4, 0:COLS])
    load("side", tokens.at[4:ROWS, 0:8], tok.at[4:ROWS, 0:8])
    load("tok", tokens.at[4:ROWS, 8:COLS], tok.at[4:ROWS, 8:COLS])
    load("fq", fine_qkv, w_fq)
    for j in range(4):
        load("cot%d" % j, cot.at[:, :, 128 * j : 128 * j + 128], cotx.at[0:ROWS, j, 0:COLS])

    def exchange(first, sent, landed, edge, corner, ahead):
        targets = ((up, lon), (lat, west), (up, west)) if ahead else ((down, lon), (lat, east), (down, east))
        sources = (sent[0], sent[1].at[edge[0] : edge[1]], sent[1].at[corner[0] : corner[1]])
        copies = []
        for i, (src, dst, (a, o)) in enumerate(zip(sources, landed, targets)):
            copies.append(pltpu.make_async_remote_copy(
                src_ref=src, dst_ref=dst, send_sem=send_sem.at[first + i], recv_sem=recv_sem.at[first + i],
                device_id={"lat": a, "lon": o}, device_id_type=MESH))
        for copy in reversed(copies):
            copy.start()
        return copies

    def pieces(value, start, size):
        return jnp.concatenate([value[8 * a + start : 8 * a + start + size] for a in range(value.shape[0] // 8)], axis=0)

    loads["top"].wait()
    loads["side"].wait()
    for i in range(4):
        tok_s[0][i] = tok[i, 0:64, :].astype(BF16)
        tok_s[1][16 * i : 16 * i + 16, :] = jnp.concatenate([tok[4 * i + e, 0:4, :] for e in range(4)], axis=0).astype(BF16)
    pl.semaphore_wait(barrier, 6)
    tok_copies = exchange(0, tok_s, tok_d, (16, 64), (0, 16), True)
    loads["tok"].wait()
    load("fp", fine_proj, w_fp)
    load("e", expand_w, w_e)
    load("m", merge_w, w_m)

    lane = lax.broadcasted_iota(jnp.int32, (1, 128), 1)
    low = lane < 64
    halves = [low.astype(F32).astype(BF16), (lane >= 64).astype(F32).astype(BF16)]
    keys = lax.broadcasted_iota(jnp.int32, (64, GROUP), 0) // 32
    queries = (lax.broadcasted_iota(jnp.int32, (64, GROUP), 1) // 32) % 2
    last = jnp.where(lat == n_lat - 1, 1, 0)
    bias[0] = jnp.zeros((64, GROUP), F32)
    bias[1] = jnp.where((keys != queries) & (last == 1), -jnp.inf, 0.0)

    def product(a, w, tiles, put):
        for n in range(tiles):
            put(n, dot(a, w[:, TILE * n : TILE * n + TILE]))

    def product_t(a, w, tiles, put):
        for n in range(tiles):
            put(n, dot_nt(a, w[TILE * n : TILE * n + TILE, :]))

    def store_to(ref, rows):
        def put(n, value):
            ref[rows, TILE * n : TILE * n + TILE] = value.astype(ref.dtype)
        return put

    def groups_of(first, windows, channels):
        for w in range(first, first + windows):
            for g in range(channels // GROUP):
                yield pl.ds(64 * w, 64), [pl.ds(c * channels + g * GROUP, GROUP) for c in range(3)]

    def attention(qkv, p_ref, out, first, windows, channels, bias_of):
        places = list(groups_of(first, windows, channels))
        items = [tuple(qkv[rows, lanes] for lanes in three) for rows, three in places]
        done = attend(items, [bias[bias_of(rows.start // 64)] for rows, three in places], halves, low)
        for (rows, three), (p, o) in zip(places, done):
            p_ref[rows, three[0]] = p
            out[rows, three[0]] = o.astype(BF16)

    def attention_grad(qkv, p_ref, d_out, first, windows, channels):
        places = list(groups_of(first, windows, channels))
        items = [tuple(qkv[rows, lanes] for lanes in three) for rows, three in places]
        probs = [p_ref[rows, three[0]] for rows, three in places]
        d_outs = [d_out[rows, three[0]] for rows, three in places]
        done = attend_grad(items, probs, d_outs, halves, low)
        for (rows, three), grads in zip(places, done):
            for lanes, value in zip(three, grads):
                qkv[rows, lanes] = value.astype(BF16)

    def window_rows(first, count):
        return slice(64 * first, 64 * (first + count))

    def x_window(w):
        return xs[8 * (w // 8) : 8 * (w // 8) + 8, 8 * (w % 8) : 8 * (w % 8) + 8, :].reshape(64, CH)

    def fine_norm(first, count):
        for w in range(first, first + count):
            (c,), scale = norm_stats([x_window(w)], CH)
            n_f[64 * w : 64 * w + 64, :] = (c * scale * fine_gain[...]).astype(BF16)

    def fine_attend(first, count):
        rows = window_rows(first, count)
        product(n_f[rows, :], w_fq, 3 * CH // TILE, store_to(qkv_f, rows))
        attention(qkv_f, p_f, m_f, first, count, CH, lambda w: w // 8)

    def fine_join(first, count):
        def put(n, value):
            lanes = slice(TILE * n, TILE * n + TILE)
            branch = value.astype(BF16).astype(F32)
            for w in range(first, first + count):
                r, c = 8 * (w // 8), 8 * (w % 8)
                own = branch[64 * (w - first) : 64 * (w - first) + 64]
                full = xs[r : r + 8, c : c + 8, lanes] + own.reshape(8, 8, TILE)
                for j in range(2):
                    fo[4 + r : 12 + r, 2 * n + j, 8 + c : 16 + c, :] = full[:, :, 128 * j : 128 * j + 128]
                if w >= 8:
                    fo_s[0][w - 8, :, lanes] = own[32:].astype(BF16)
                if w % 8 == 7:
                    fo_s[1][32 * (w // 8) : 32 * (w // 8) + 32, lanes] = pieces(own, 4, 4).astype(BF16)
        product(m_f[window_rows(first, count), :], w_fp, CH // TILE, put)

    def spread(ref, row, start, count):
        return jnp.concatenate([ref[row, j, pl.ds(start, count, stride=2), :] for j in range(4)], axis=1)

    def merged(row, col, count):
        return [spread(fo, 4 + 2 * row + a, 8 + 2 * col + b, count) for a in range(2) for b in range(2)]

    batch_a = [(i, 0, 32, 32 * i) for i in range(4)] + [(4 + i, 0, 16, 128 + 16 * i) for i in range(4)]
    batch_b = [(4 + i, 16, 16, 192 + 16 * i) for i in range(4)]

    for i in range(8):
        xs[i, 0:56, :] = tok[i + 4, 4:60, :]
    fine_norm(0, 7)
    for j in range(4):
        loads["cot%d" % j].wait()
    for i in range(4):
        for j in range(4):
            cot_s[0][i, j] = cotx[i, j, 0:64, :].astype(BF16)
            cot_s[1][i, j] = jnp.concatenate([cotx[4 * i + e, j, 0:4, :] for e in range(4)], axis=0).astype(BF16)
    cot_copies = exchange(3, cot_s, cot_d, (1, 4), (0, 1), True)
    loads["fq"].wait()
    fine_attend(0, 7)
    load("cq", coarse_qkv, w_cq)
    load("cp", coarse_proj, w_cp)
    loads["fp"].wait()
    fine_join(0, 7)
    for i in range(8):
        for a in range(2):
            for b in range(2):
                part = 2 * a + b
                cells[32 * i : 32 * i + 32, CH * part : CH * (part + 1)] = spread(cotx, 2 * i + a, b, 32).astype(BF16)
    loads["e"].wait()
    everything = slice(0, 256)
    def put_dco(n, value):
        lanes = slice(TILE * n, TILE * n + TILE)
        dco_s[0][:, :, lanes] = value[0:128].reshape(4, 32, TILE).astype(BF16)
        dco_s[1][:, lanes] = jnp.concatenate([value[32 * i : 32 * i + 4] for i in range(8)], axis=0).astype(BF16)
        co[0:4, 0:32, lanes] = value[128:256].reshape(4, 32, TILE)
    product_t(cells[...], w_e, WIDE // TILE, put_dco)
    dco_copies = exchange(21, dco_s, dco_d, (16, 32), (0, 16), True)
    for c in tok_copies:
        c.wait_recv()
    for i in range(4):
        tok[16 + i, 0:64, :] = tok_d[0][i].astype(F32)
    for i in range(1, 4):
        side = tok_d[1][16 * i - 16 : 16 * i, :].astype(F32)
        for e in range(4):
            tok[4 * i + e, 64:68, :] = side[4 * e : 4 * e + 4]
    side = tok_d[2][...].astype(F32)
    for e in range(4):
        tok[16 + e, 64:68, :] = side[4 * e : 4 * e + 4]
    for i in range(8):
        xs[i, 56:64, :] = tok[i + 4, 60:68, :]
        xs[8 + i] = tok[i + 12, 4:68, :]
    fine_norm(7, 5)
    fine_attend(7, 5)
    fine_join(7, 5)
    def merge_norm(batch):
        for row, col, count, at in batch:
            parts, scale = norm_stats(merged(row, col, count), 4 * CH)
            for j, c in enumerate(parts):
                gain = merge_gain[:, CH * j : CH * (j + 1)]
                cells[at : at + count, CH * j : CH * (j + 1)] = (c * scale * gain).astype(BF16)
    merge_norm(batch_a)
    loads["m"].wait()
    def put_cin(n, value):
        lanes = slice(TILE * n, TILE * n + TILE)
        cin[0:4, 0:32, lanes] = value[0:128].reshape(4, 32, TILE)
        cin[4:8, 0:16, lanes] = value[128:192].reshape(4, 16, TILE)
        cin_s[0][:, :, lanes] = value[0:64].reshape(2, 32, TILE).astype(BF16)
        starts = [32 * i for i in range(4)] + [128 + 16 * i for i in range(4)]
        cin_s[1][:, lanes] = jnp.concatenate([value[i : i + 2] for i in starts], axis=0).astype(BF16)
    product(cells[0:192, :], w_m, WIDE // TILE, put_cin)
    cin_copies = exchange(6, cin_s, cin_d, (0, 16), (0, 16), True)
    fine_norm(12, 4)
    fine_attend(12, 4)
    fine_join(12, 4)
    merge_norm(batch_b)
    def put_cin_b(n, value):
        cin[4:8, 16:32, TILE * n : TILE * n + TILE] = value.reshape(4, 16, TILE)
    product(cells[192:256, :], w_m, WIDE // TILE, put_cin_b)

    for c in dco_copies:
        c.wait_recv()
    for i in range(4):
        co[4 + i, 0:32, :] = dco_d[0][i].astype(F32)
    side, tip = dco_d[1][...].astype(F32), dco_d[2][...].astype(F32)
    for i in range(4):
        co[i, 32:36, :] = side[4 * i : 4 * i + 4]
        co[4 + i, 32:36, :] = tip[4 * i : 4 * i + 4]
    for w in range(4):
        dco[64 * w : 64 * w + 64, :] = co[0:8, 4 + 8 * w : 12 + 8 * w, :].reshape(64, WIDE).astype(BF16)
    loads["cp"].wait()
    product_t(dco[...], w_cp, WIDE // TILE, store_to(dm_c, everything))

    cin_copies[0].wait_recv()
    for i in range(2):
        cin[8 + i, 0:32, :] = cin_d[0][i].astype(F32)
    def coarse_norm(w):
        x = cin[2:10, 2 + 8 * w : 10 + 8 * w, :].reshape(64, WIDE)
        xc[64 * w : 64 * w + 64, :] = x
        (c,), scale = norm_stats([x], WIDE)
        n_c[64 * w : 64 * w + 64, :] = (c * scale * coarse_gain[...]).astype(BF16)
    for w in range(3):
        coarse_norm(w)
    for c in cin_copies[1:]:
        c.wait_recv()
    fo_copies = exchange(9, fo_s, fo_d, (0, 48), (48, 64), False)
    side, tip = cin_d[1][...].astype(F32), cin_d[2][...].astype(F32)
    for i in range(2, 8):
        cin[i, 32:34, :] = side[2 * i : 2 * i + 2]
    for i in range(2):
        cin[8 + i, 32:34, :] = tip[2 * i : 2 * i + 2]
    coarse_norm(3)
    loads["cq"].wait()
    product(n_c[...], w_cq, 3 * WIDE // TILE, store_to(qkv_c, everything))
    attention(qkv_c, p_c, m_c, 0, 4, WIDE, lambda w: 1)
    def put_co(n, value):
        lanes = aligned(n, TILE)
        full = xc[:, lanes] + value.astype(BF16).astype(F32)
        for w in range(4):
            own = full[64 * w : 64 * w + 64]
            co[4:12, 8 + 8 * w : 16 + 8 * w, lanes] = own.reshape(8, 8, TILE)
            co_s[0][w, :, lanes] = own[32:].astype(BF16)
        co_s[1][:, lanes] = pieces(own, 4, 4).astype(BF16)
    product(m_c[...], w_cp, WIDE // TILE, put_co)
    co_copies = exchange(12, co_s, co_d, (0, 16), (16, 32), False)

    attention_grad(qkv_c, p_c, dm_c, 0, 4, WIDE)
    product_t(qkv_c[...], w_cq, WIDE // TILE, store_to(n_c, everything))
    for w in range(4):
        rows = slice(64 * w, 64 * w + 64)
        (d,) = norm_grad([xc[rows, :]], [n_c[rows, :].astype(F32)], [coarse_gain[...]], WIDE)
        full = d + dco[rows, :].astype(F32)
        gci[2:10, 8 + 8 * w : 16 + 8 * w, :] = full.reshape(8, 8, WIDE)
        gci_s[0][w] = full[48:].astype(BF16)
    gci_s[1][...] = pieces(full, 6, 2).astype(BF16)
    gci_copies = exchange(15, gci_s, gci_d, (0, 16), (0, 16), False)

    def merge_grad(batch):
        first, last = batch[0][3], batch[-1][3] + batch[-1][2]
        for row, col, count, at in batch:
            n_c[at : at + count, :] = gci[row, 6 + col : 6 + col + count, :].astype(BF16)
        product_t(n_c[first:last, :], w_m, 4 * CH // TILE, store_to(cells, slice(first, last)))
        gains = [merge_gain[:, CH * j : CH * (j + 1)] for j in range(4)]
        for row, col, count, at in batch:
            grads = [cells[at : at + count, CH * j : CH * (j + 1)].astype(F32) for j in range(4)]
            done = norm_grad(merged(row, col, count), grads, gains, 4 * CH)
            for a in range(2):
                for b in range(2):
                    full = spread(cotx, 4 + 2 * row + a, 4 + 2 * col + b, count) + done[2 * a + b]
                    for j in range(4):
                        gf[2 * row + a, j, pl.ds(2 * col + b, count, stride=2), :] = full[:, 128 * j : 128 * j + 128]

    def window(wr, w):
        return jnp.concatenate(
            [gf[8 * wr : 8 * wr + 8, j, aligned(w, 8), :].reshape(64, 128) for j in range(4)], axis=1)
    gt = tok
    def fine_grad(first, count):
        rows = window_rows(first, count)
        for w in range(first, first + count):
            n_f[64 * w : 64 * w + 64, :] = window(w // 8, w % 8).astype(BF16)
        product_t(n_f[rows, :], w_fp, CH // TILE, store_to(m_f, rows))
        attention_grad(qkv_f, p_f, m_f, first, count, CH)
        product_t(qkv_f[rows, :], w_fq, CH // TILE, store_to(n_f, rows))
        for w in range(first, first + count):
            dn = n_f[64 * w : 64 * w + 64, :].astype(F32)
            (d,) = norm_grad([x_window(w)], [dn], [fine_gain[...]], CH)
            full = window(w // 8, w % 8) + d
            r, c = 8 * (w // 8), 8 * (w % 8)
            gt[4 + r : 12 + r, 8 + c : 16 + c, :] = full.reshape(8, 8, CH)
            if w >= 8:
                gt_s[0][w - 8] = full[32:].astype(BF16)
            if w % 8 == 7:
                gt_s[1][32 * (w // 8) : 32 * (w // 8) + 32, :] = pieces(full, 4, 4).astype(BF16)
    for c in cot_copies:
        c.wait_recv()
    for i in range(4):
        for j in range(4):
            cotx[16 + i, j, 0:64, :] = cot_d[0][i, j].astype(F32)
    for i in range(1, 5):
        for j in range(4):
            side = (cot_d[1][i - 1, j] if i < 4 else cot_d[2][0, j]).astype(F32)
            for e in range(4):
                cotx[4 * i + e, j, 64:68, :] = side[4 * e : 4 * e + 4]
    merge_grad(batch_b)
    fine_grad(12, 4)
    gt_first = pltpu.make_async_remote_copy(
        src_ref=gt_s[0].at[4:8], dst_ref=gt_d[0].at[4:8], send_sem=send_sem.at[24], recv_sem=recv_sem.at[24],
        device_id={"lat": down, "lon": lon}, device_id_type=MESH)
    gt_first.start()
    for c in fo_copies:
        c.wait_recv()
    for w in range(8):
        strip = fo_d[0][w].astype(F32)
        for a in range(4):
            full = tok[a, 4 + 8 * w : 12 + 8 * w, :] + strip[8 * a : 8 * a + 8]
            for j in range(4):
                fo[a, j, 8 + 8 * w : 16 + 8 * w, :] = full[:, 128 * j : 128 * j + 128]
    side, tip = fo_d[1][...].astype(F32), fo_d[2][...].astype(F32)
    for a in range(16):
        full = tok[a, 0:4, :] + (tip[4 * a : 4 * a + 4] if a < 4 else side[4 * a - 16 : 4 * a - 12])
        for j in range(4):
            fo[a, j, 4:8, :] = full[:, 128 * j : 128 * j + 128]
    for c in co_copies:
        c.wait_recv()
    for w in range(4):
        strip = co_d[0][w].astype(F32)
        for a in range(4):
            co[a, 8 + 8 * w : 16 + 8 * w, :] = strip[8 * a : 8 * a + 8]
    side, tip = co_d[1][...].astype(F32), co_d[2][...].astype(F32)
    for a in range(4):
        co[a, 4:8, :] = tip[4 * a : 4 * a + 4]
        co[4 + a, 4:8, :] = side[4 * a : 4 * a + 4]
    for i in range(8):
        n_c[32 * i : 32 * i + 32, :] = co[i, 4:36, :].astype(BF16)
    for a in range(2):
        for b in range(2):
            part = 2 * a + b
            def lift(n, carry):
                w = w_e[:, pl.ds(part * CH + n * TILE, TILE)]
                lifted = dot(n_c[...], w)
                for s in range(2):
                    j = 2 * n + s
                    for i in range(8):
                        part_fo = fo[2 * i + a, j, pl.ds(4 + b, 32, stride=2), :]
                        res[2 * i + a, j, pl.ds(b, 32, stride=2), :] = part_fo + lifted[32 * i : 32 * i + 32, 128 * s : 128 * s + 128]
                return carry
            unrolled(0, CH // TILE, lift)
    out_result = [
        pltpu.make_async_copy(res.at[:, j], result.at[:, :, 128 * j : 128 * j + 128], load_sem.at[14 + j])
        for j in range(4)
    ]
    for c in out_result:
        c.start()

    for c in gci_copies:
        c.wait_recv()
    for w in range(4):
        strip = gci_d[0][w].astype(F32)
        for a in range(2):
            gci[a, 8 + 8 * w : 16 + 8 * w, :] = strip[8 * a : 8 * a + 8]
    side, tip = gci_d[1][...].astype(F32), gci_d[2][...].astype(F32)
    for a in range(6):
        gci[2 + a, 6:8, :] = side[2 * a : 2 * a + 2]
    for a in range(2):
        gci[a, 6:8, :] = tip[12 + 2 * a : 14 + 2 * a]
    merge_grad(batch_a)
    fine_grad(7, 5)
    gt_copies = exchange(
        18, (gt_s[0].at[0:4], gt_s[1]), (gt_d[0].at[0:4], gt_d[1], gt_d[2]), (0, 48), (48, 64), False)
    fine_grad(0, 7)
    for i in range(4, ROWS):
        xs[i, 8:64, :] = gt[i, 12:68, :]
    out_grad = [
        pltpu.make_async_copy(xs.at[rows, cols], grad.at[rows, cols], load_sem.at[slot])
        for rows, cols, slot in (
            (pl.ds(4, 12), pl.ds(8, 56), 13), (pl.ds(4, 12), pl.ds(0, 8), 18), (pl.ds(0, 4), pl.ds(0, 64), 19))
    ]
    out_grad[0].start()
    gt_copies.append(gt_first)
    for c in gt_copies:
        c.wait_recv()
    side, tip = gt_d[1][...].astype(F32), gt_d[2][...].astype(F32)
    for a in range(16):
        gt[a, 4:8, :] = tip[4 * a : 4 * a + 4] if a < 4 else side[4 * a - 16 : 4 * a - 12]
    for i in range(4, ROWS):
        xs[i, 0:8, :] = gt[i, 4:12, :]
    out_grad[1].start()
    for w in range(8):
        strip = gt_d[0][w].astype(F32)
        for a in range(4):
            gt[a, 8 + 8 * w : 16 + 8 * w, :] = strip[8 * a : 8 * a + 8]
    for i in range(4):
        xs[i] = gt[i, 4:68, :]
    out_grad[2].start()
    for c in tok_copies + cot_copies + dco_copies + cin_copies + fo_copies + co_copies + gci_copies + gt_copies:
        c.wait_send()
    for c in out_result + out_grad:
        c.wait()


def exchanged(strip, side, edge, corner):
    vmem = pltpu.VMEM
    return (
        (vmem(strip, BF16), vmem(side, BF16)),
        (vmem(strip, BF16), vmem((edge,) + side[1:], BF16), vmem((corner,) + side[1:], BF16)),
    )


def local(
    tokens, fine_gain, fine_qkv, fine_proj, merge_gain, merge_weight,
    coarse_gain, coarse_qkv, coarse_proj, expand_weight, cotangent,
):
    vmem = pltpu.VMEM
    shape = jax.ShapeDtypeStruct((ROWS, COLS, CH), F32)
    hbm = pl.BlockSpec(memory_space=pl.ANY)
    whole = pl.BlockSpec(memory_space=pltpu.VMEM)
    done = pl.pallas_call(
        kernel,
        out_shape=(shape, shape),
        in_specs=[hbm, hbm, whole, whole, whole] + [hbm] * 6,
        out_specs=(hbm, hbm),
        scratch_shapes=[
            vmem((20, 72, CH), F32),
            vmem((20, 4, 72, 128), F32),
            vmem((ROWS, COLS, CH), F32),
            vmem((20, 4, 72, 128), F32),
            vmem((10, 40, WIDE), F32),
            vmem((10, 40, WIDE), F32),
            vmem((12, 40, WIDE), F32),
            vmem((256, WIDE), F32),
            vmem((ROWS, 4, COLS, 128), F32),
            vmem((ROWS, 4, COLS, 128), F32),
            vmem((1024, 3 * CH), BF16),
            vmem((1024, CH), F32),
            vmem((256, 3 * WIDE), BF16),
            vmem((256, WIDE), F32),
            vmem((1024, CH), BF16),
            vmem((1024, CH), BF16),
            vmem((256, 4 * CH), BF16),
            vmem((256, WIDE), BF16),
            vmem((256, WIDE), BF16),
            vmem((256, WIDE), BF16),
            vmem((256, WIDE), BF16),
            vmem((2, 64, GROUP), F32),
            vmem(fine_qkv.shape, BF16),
            vmem(fine_proj.shape, BF16),
            vmem(merge_weight.shape, BF16),
            vmem(coarse_qkv.shape, BF16),
            vmem(coarse_proj.shape, BF16),
            vmem(expand_weight.shape, BF16),
            *exchanged((4, 64, CH), (64, CH), 48, 16),
            *exchanged((4, 4, 64, 128), (4, 4, 16, 128), 3, 1),
            *exchanged((4, 32, WIDE), (32, WIDE), 16, 16),
            *exchanged((2, 32, WIDE), (16, WIDE), 16, 16),
            *exchanged((8, 32, CH), (64, CH), 48, 16),
            *exchanged((4, 32, WIDE), (32, WIDE), 16, 16),
            *exchanged((4, 16, WIDE), (16, WIDE), 16, 16),
            *exchanged((8, 32, CH), (64, CH), 48, 16),
            pltpu.SemaphoreType.DMA((20,)),
            pltpu.SemaphoreType.DMA((25,)),
            pltpu.SemaphoreType.DMA((25,)),
        ],
        compiler_params=pltpu.CompilerParams(
            collective_id=0, has_side_effects=True, vmem_limit_bytes=63 * 1024 * 1024),
    )(
        tokens, cotangent, fine_gain.reshape(1, -1), merge_gain.reshape(1, -1), coarse_gain.reshape(1, -1),
        fine_qkv, fine_proj, merge_weight, coarse_qkv, coarse_proj, expand_weight,
    )
    return pl.pallas_call(
        hand_over,
        out_shape=(shape, shape),
        in_specs=[hbm, hbm],
        out_specs=(hbm, hbm),
        scratch_shapes=[
            pltpu.VMEM((8, 4, COLS, CH), F32), pltpu.SemaphoreType.DMA((8,)), pltpu.SemaphoreType.DMA((8,))],
    )(*done)


def hand_over(result, grad, result_out, grad_out, held, load_sem, store_sem):
    loads, stores = [], []
    for i, (src, dst) in enumerate(((result, result_out), (grad, grad_out))):
        for part in range(4):
            rows, slot = pl.ds(4 * part, 4), 4 * i + part
            loads.append(pltpu.make_async_copy(src.at[rows], held.at[slot], load_sem.at[slot]))
            stores.append(pltpu.make_async_copy(held.at[slot], dst.at[rows], store_sem.at[slot]))
            loads[-1].start()
    for load, store in zip(loads, stores):
        load.wait()
        store.start()
    for store in stores:
        store.wait()


def solution(mesh):
    field = P("lat", "lon", None)
    placed = (field,) + (P(),) * 9 + (field,)
    return jax.shard_map(local, mesh=mesh, in_specs=placed, out_specs=(field, field), check_vma=False)
```

```python
import functools
import math

import jax
import jax.numpy as jnp
from jax import lax
from jax.experimental import pallas as pl
from jax.experimental.pallas import tpu as pltpu
from jax.sharding import PartitionSpec as P

F32 = jnp.float32
BF16 = jnp.bfloat16
MESH = pl.DeviceIdType.MESH

ROWS, COLS, CH = 16, 64, 512
CROWS, CCOLS, WIDE = 8, 32, 1024
HEAD = 64
GROUP = 256
TILE = 256
EXP_SCALE = math.log2(math.e) / math.sqrt(HEAD)


def dot(a, b):
    return jnp.dot(a, b, preferred_element_type=F32)


def dot_nt(a, b):
    return lax.dot_general(a, b, (((1,), (1,)), ((), ())), preferred_element_type=F32)


def dot_tn(a, b):
    return lax.dot_general(a, b, (((0,), (0,)), ((), ())), preferred_element_type=F32)


def norm_stats(parts, width):
    mean = sum(jnp.sum(p, axis=-1, keepdims=True) for p in parts) * (1.0 / width)
    centred = [p - mean for p in parts]
    spread = sum(jnp.sum(c * c, axis=-1, keepdims=True) for c in centred) * (1.0 / width)
    return centred, lax.rsqrt(spread + 1e-05)


def norm_grad(parts, grads, gains, width):
    centred, scale = norm_stats(parts, width)
    xhat = [c * scale for c in centred]
    gy = [d * g for d, g in zip(grads, gains)]
    first = sum(jnp.sum(y, axis=-1, keepdims=True) for y in gy) * (1.0 / width)
    second = sum(jnp.sum(y * x, axis=-1, keepdims=True) for y, x in zip(gy, xhat)) * (1.0 / width)
    return [scale * (y - first - x * second) for y, x in zip(gy, xhat)]


def block_diagonal(x, halves):
    zero = jnp.zeros((64, 128), BF16)
    rows = []
    for h in range(4):
        piece = x[:, 128 * (h // 2) : 128 * (h // 2) + 128] * halves[h % 2]
        rows.append(jnp.concatenate([piece, zero] if h < 2 else [zero, piece], axis=1))
    return jnp.concatenate(rows, axis=0)


def per_query(weights, values, low):
    out = []
    for t in range(2):
        lanes = slice(128 * t, 128 * t + 128)
        full = dot_tn(weights[:, lanes], values[:, lanes])
        out.append(jnp.where(low, full[:64], full[64:]))
    return jnp.concatenate(out, axis=1)


def attend(items, biases, halves, low):
    scores = [dot_nt(k, block_diagonal(q, halves)) + b for (q, k, v), b in zip(items, biases)]
    probs = []
    for s in scores:
        e = jnp.exp2((s - jnp.max(s, axis=0, keepdims=True)) * EXP_SCALE)
        probs.append(e * (1.0 / jnp.sum(e, axis=0, keepdims=True)))
    return [(p, per_query(p.astype(BF16), v, low)) for p, (q, k, v) in zip(probs, items)]


def attend_grad(items, probs, d_outs, halves, low):
    d_diags = [block_diagonal(d, halves) for d in d_outs]
    dps = [dot_nt(v, d) for (q, k, v), d in zip(items, d_diags)]
    dvs = [dot(p.astype(BF16), d) for p, d in zip(probs, d_diags)]
    dss = []
    for p, dp in zip(probs, dps):
        weighted = p * dp
        dss.append(((weighted - p * jnp.sum(weighted, axis=0, keepdims=True)) * (1.0 / math.sqrt(HEAD))).astype(BF16))
    dks = [dot(ds, block_diagonal(q, halves)) for ds, (q, k, v) in zip(dss, items)]
    dqs = [per_query(ds, k, low) for ds, (q, k, v) in zip(dss, items)]
    return list(zip(dqs, dks, dvs))


def aligned(i, step):
    return pl.ds(i * step, step)


def unrolled(first, last, step):
    for i in range(first, last):
        step(i, 0)


def kernel(
    tokens, cot, fine_gain, merge_gain, coarse_gain,
    fine_qkv, fine_proj, merge_w, coarse_qkv, coarse_proj, expand_w,
    result, grad,
    tok, cotx, xs, fo, cin, gci, co, xc, gf, res,
    qkv_f, p_f, qkv_c, p_c, n_f, m_f, cells, n_c, m_c, dm_c, dco, bias,
    w_fq, w_fp, w_m, w_cq, w_cp, w_e,
    tok_s, tok_d, cot_s, cot_d, dco_s, dco_d, cin_s, cin_d, fo_s, fo_d, co_s, co_d, gci_s, gci_d, gt_s, gt_d,
    load_sem, send_sem, recv_sem,
):
    lat, lon = lax.axis_index("lat"), lax.axis_index("lon")
    n_lat, n_lon = lax.axis_size("lat"), lax.axis_size("lon")
    up, down = lax.rem(lat + n_lat - 1, n_lat), lax.rem(lat + 1, n_lat)
    west, east = lax.rem(lon + n_lon - 1, n_lon), lax.rem(lon + 1, n_lon)

    barrier = pltpu.get_barrier_semaphore()
    for a, o in ((up, lon), (lat, west), (up, west), (down, lon), (lat, east), (down, east)):
        pl.semaphore_signal(barrier, inc=1, device_id={"lat": a, "lon": o}, device_id_type=MESH)

    loads = {}
    def load(name, src, dst):
        loads[name] = pltpu.make_async_copy(src, dst, load_sem.at[len(loads)])
        loads[name].start()

    load("top", tokens.at[0:4], tok.at[0:4, 0:COLS])
    load("side", tokens.at[4:ROWS, 0:8], tok.at[4:ROWS, 0:8])
    load("tok", tokens.at[4:ROWS, 8:COLS], tok.at[4:ROWS, 8:COLS])
    load("fq", fine_qkv, w_fq)
    for j in range(4):
        load("cot%d" % j, cot.at[:, :, 128 * j : 128 * j + 128], cotx.at[0:ROWS, j, 0:COLS])

    def exchange(first, sent, landed, edge, corner, ahead):
        targets = ((up, lon), (lat, west), (up, west)) if ahead else ((down, lon), (lat, east), (down, east))
        sources = (sent[0], sent[1].at[edge[0] : edge[1]], sent[1].at[corner[0] : corner[1]])
        copies = []
        for i, (src, dst, (a, o)) in enumerate(zip(sources, landed, targets)):
            copies.append(pltpu.make_async_remote_copy(
                src_ref=src, dst_ref=dst, send_sem=send_sem.at[first + i], recv_sem=recv_sem.at[first + i],
                device_id={"lat": a, "lon": o}, device_id_type=MESH))
        for copy in reversed(copies):
            copy.start()
        return copies

    def pieces(value, start, size):
        return jnp.concatenate([value[8 * a + start : 8 * a + start + size] for a in range(value.shape[0] // 8)], axis=0)

    loads["top"].wait()
    loads["side"].wait()
    for i in range(4):
        tok_s[0][i] = tok[i, 0:64, :].astype(BF16)
        tok_s[1][16 * i : 16 * i + 16, :] = jnp.concatenate([tok[4 * i + e, 0:4, :] for e in range(4)], axis=0).astype(BF16)
    pl.semaphore_wait(barrier, 6)
    tok_copies = exchange(0, tok_s, tok_d, (16, 64), (0, 16), True)
    loads["tok"].wait()
    load("fp", fine_proj, w_fp)
    load("e", expand_w, w_e)
    load("m", merge_w, w_m)

    lane = lax.broadcasted_iota(jnp.int32, (1, 128), 1)
    low = lane < 64
    halves = [low.astype(F32).astype(BF16), (lane >= 64).astype(F32).astype(BF16)]
    keys = lax.broadcasted_iota(jnp.int32, (64, GROUP), 0) // 32
    queries = (lax.broadcasted_iota(jnp.int32, (64, GROUP), 1) // 32) % 2
    last = jnp.where(lat == n_lat - 1, 1, 0)
    bias[0] = jnp.zeros((64, GROUP), F32)
    bias[1] = jnp.where((keys != queries) & (last == 1), -jnp.inf, 0.0)

    def product(a, w, tiles, put):
        for n in range(tiles):
            put(n, dot(a, w[:, TILE * n : TILE * n + TILE]))

    def product_t(a, w, tiles, put):
        for n in range(tiles):
            put(n, dot_nt(a, w[TILE * n : TILE * n + TILE, :]))

    def store_to(ref, rows):
        def put(n, value):
            ref[rows, TILE * n : TILE * n + TILE] = value.astype(ref.dtype)
        return put

    def groups_of(first, windows, channels):
        for w in range(first, first + windows):
            for g in range(channels // GROUP):
                yield pl.ds(64 * w, 64), [pl.ds(c * channels + g * GROUP, GROUP) for c in range(3)]

    def attention(qkv, p_ref, out, first, windows, channels, bias_of):
        places = list(groups_of(first, windows, channels))
        items = [tuple(qkv[rows, lanes] for lanes in three) for rows, three in places]
        done = attend(items, [bias[bias_of(rows.start // 64)] for rows, three in places], halves, low)
        for (rows, three), (p, o) in zip(places, done):
            p_ref[rows, three[0]] = p
            out[rows, three[0]] = o.astype(BF16)

    def attention_grad(qkv, p_ref, d_out, first, windows, channels):
        places = list(groups_of(first, windows, channels))
        items = [tuple(qkv[rows, lanes] for lanes in three) for rows, three in places]
        probs = [p_ref[rows, three[0]] for rows, three in places]
        d_outs = [d_out[rows, three[0]] for rows, three in places]
        done = attend_grad(items, probs, d_outs, halves, low)
        for (rows, three), grads in zip(places, done):
            for lanes, value in zip(three, grads):
                qkv[rows, lanes] = value.astype(BF16)

    def window_rows(first, count):
        return slice(64 * first, 64 * (first + count))

    def x_window(w):
        return xs[8 * (w // 8) : 8 * (w // 8) + 8, 8 * (w % 8) : 8 * (w % 8) + 8, :].reshape(64, CH)

    def fine_norm(first, count):
        for w in range(first, first + count):
            (c,), scale = norm_stats([x_window(w)], CH)
            n_f[64 * w : 64 * w + 64, :] = (c * scale * fine_gain[...]).astype(BF16)

    def fine_attend(first, count):
        rows = window_rows(first, count)
        product(n_f[rows, :], w_fq, 3 * CH // TILE, store_to(qkv_f, rows))
        attention(qkv_f, p_f, m_f, first, count, CH, lambda w: w // 8)

    def fine_join(first, count):
        def put(n, value):
            lanes = slice(TILE * n, TILE * n + TILE)
            branch = value.astype(BF16).astype(F32)
            for w in range(first, first + count):
                r, c = 8 * (w // 8), 8 * (w % 8)
                own = branch[64 * (w - first) : 64 * (w - first) + 64]
                full = xs[r : r + 8, c : c + 8, lanes] + own.reshape(8, 8, TILE)
                for j in range(2):
                    fo[4 + r : 12 + r, 2 * n + j, 8 + c : 16 + c, :] = full[:, :, 128 * j : 128 * j + 128]
                if w >= 8:
                    fo_s[0][w - 8, :, lanes] = own[32:].astype(BF16)
                if w % 8 == 7:
                    fo_s[1][32 * (w // 8) : 32 * (w // 8) + 32, lanes] = pieces(own, 4, 4).astype(BF16)
        product(m_f[window_rows(first, count), :], w_fp, CH // TILE, put)

    def spread(ref, row, start, count):
        return jnp.concatenate([ref[row, j, pl.ds(start, count, stride=2), :] for j in range(4)], axis=1)

    def merged(row, col, count):
        return [spread(fo, 4 + 2 * row + a, 8 + 2 * col + b, count) for a in range(2) for b in range(2)]

    batch_a = [(i, 0, 32, 32 * i) for i in range(4)] + [(4 + i, 0, 16, 128 + 16 * i) for i in range(4)]
    batch_b = [(4 + i, 16, 16, 192 + 16 * i) for i in range(4)]

    for i in range(8):
        xs[i, 0:56, :] = tok[i + 4, 4:60, :]
    fine_norm(0, 7)
    loads["fq"].wait()
    fine_attend(0, 7)
    for j in range(4):
        loads["cot%d" % j].wait()
    for i in range(4):
        for j in range(4):
            cot_s[0][i, j] = cotx[i, j, 0:64, :].astype(BF16)
            cot_s[1][i, j] = jnp.concatenate([cotx[4 * i + e, j, 0:4, :] for e in range(4)], axis=0).astype(BF16)
    cot_copies = exchange(3, cot_s, cot_d, (1, 4), (0, 1), True)
    load("cq", coarse_qkv, w_cq)
    load("cp", coarse_proj, w_cp)
    loads["fp"].wait()
    fine_join(0, 7)
    for i in range(8):
        for a in range(2):
            for b in range(2):
                part = 2 * a + b
                cells[32 * i : 32 * i + 32, CH * part : CH * (part + 1)] = spread(cotx, 2 * i + a, b, 32).astype(BF16)
    loads["e"].wait()
    everything = slice(0, 256)
    def put_dco(n, value):
        lanes = slice(TILE * n, TILE * n + TILE)
        dco_s[0][:, :, lanes] = value[0:128].reshape(4, 32, TILE).astype(BF16)
        dco_s[1][:, lanes] = jnp.concatenate([value[32 * i : 32 * i + 4] for i in range(8)], axis=0).astype(BF16)
        co[0:4, 0:32, lanes] = value[128:256].reshape(4, 32, TILE)
    product_t(cells[...], w_e, WIDE // TILE, put_dco)
    dco_copies = exchange(21, dco_s, dco_d, (16, 32), (0, 16), True)
    for c in tok_copies:
        c.wait_recv()
    for i in range(4):
        tok[16 + i, 0:64, :] = tok_d[0][i].astype(F32)
    for i in range(1, 4):
        side = tok_d[1][16 * i - 16 : 16 * i, :].astype(F32)
        for e in range(4):
            tok[4 * i + e, 64:68, :] = side[4 * e : 4 * e + 4]
    side = tok_d[2][...].astype(F32)
    for e in range(4):
        tok[16 + e, 64:68, :] = side[4 * e : 4 * e + 4]
    for i in range(8):
        xs[i, 56:64, :] = tok[i + 4, 60:68, :]
        xs[8 + i] = tok[i + 12, 4:68, :]
    fine_norm(7, 5)
    fine_attend(7, 5)
    fine_join(7, 5)
    def merge_norm(batch):
        for row, col, count, at in batch:
            parts, scale = norm_stats(merged(row, col, count), 4 * CH)
            for j, c in enumerate(parts):
                gain = merge_gain[:, CH * j : CH * (j + 1)]
                cells[at : at + count, CH * j : CH * (j + 1)] = (c * scale * gain).astype(BF16)
    merge_norm(batch_a)
    loads["m"].wait()
    def put_cin(n, value):
        lanes = slice(TILE * n, TILE * n + TILE)
        cin[0:4, 0:32, lanes] = value[0:128].reshape(4, 32, TILE)
        cin[4:8, 0:16, lanes] = value[128:192].reshape(4, 16, TILE)
        cin_s[0][:, :, lanes] = value[0:64].reshape(2, 32, TILE).astype(BF16)
        starts = [32 * i for i in range(4)] + [128 + 16 * i for i in range(4)]
        cin_s[1][:, lanes] = jnp.concatenate([value[i : i + 2] for i in starts], axis=0).astype(BF16)
    product(cells[0:192, :], w_m, WIDE // TILE, put_cin)
    cin_copies = exchange(6, cin_s, cin_d, (0, 16), (0, 16), True)
    fine_norm(12, 4)
    fine_attend(12, 4)
    fine_join(12, 4)
    merge_norm(batch_b)
    def put_cin_b(n, value):
        cin[4:8, 16:32, TILE * n : TILE * n + TILE] = value.reshape(4, 16, TILE)
    product(cells[192:256, :], w_m, WIDE // TILE, put_cin_b)

    for c in dco_copies:
        c.wait_recv()
    for i in range(4):
        co[4 + i, 0:32, :] = dco_d[0][i].astype(F32)
    side, tip = dco_d[1][...].astype(F32), dco_d[2][...].astype(F32)
    for i in range(4):
        co[i, 32:36, :] = side[4 * i : 4 * i + 4]
        co[4 + i, 32:36, :] = tip[4 * i : 4 * i + 4]
    for w in range(4):
        dco[64 * w : 64 * w + 64, :] = co[0:8, 4 + 8 * w : 12 + 8 * w, :].reshape(64, WIDE).astype(BF16)
    loads["cp"].wait()
    product_t(dco[...], w_cp, WIDE // TILE, store_to(dm_c, everything))

    cin_copies[0].wait_recv()
    for i in range(2):
        cin[8 + i, 0:32, :] = cin_d[0][i].astype(F32)
    def coarse_norm(w):
        x = cin[2:10, 2 + 8 * w : 10 + 8 * w, :].reshape(64, WIDE)
        xc[64 * w : 64 * w + 64, :] = x
        (c,), scale = norm_stats([x], WIDE)
        n_c[64 * w : 64 * w + 64, :] = (c * scale * coarse_gain[...]).astype(BF16)
    for w in range(3):
        coarse_norm(w)
    for c in cin_copies[1:]:
        c.wait_recv()
    fo_copies = exchange(9, fo_s, fo_d, (0, 48), (48, 64), False)
    side, tip = cin_d[1][...].astype(F32), cin_d[2][...].astype(F32)
    for i in range(2, 8):
        cin[i, 32:34, :] = side[2 * i : 2 * i + 2]
    for i in range(2):
        cin[8 + i, 32:34, :] = tip[2 * i : 2 * i + 2]
    coarse_norm(3)
    loads["cq"].wait()
    product(n_c[...], w_cq, 3 * WIDE // TILE, store_to(qkv_c, everything))
    attention(qkv_c, p_c, m_c, 0, 4, WIDE, lambda w: 1)
    def put_co(n, value):
        lanes = aligned(n, TILE)
        full = xc[:, lanes] + value.astype(BF16).astype(F32)
        for w in range(4):
            own = full[64 * w : 64 * w + 64]
            co[4:12, 8 + 8 * w : 16 + 8 * w, lanes] = own.reshape(8, 8, TILE)
            co_s[0][w, :, lanes] = own[32:].astype(BF16)
        co_s[1][:, lanes] = pieces(own, 4, 4).astype(BF16)
    product(m_c[...], w_cp, WIDE // TILE, put_co)
    co_copies = exchange(12, co_s, co_d, (0, 16), (16, 32), False)

    attention_grad(qkv_c, p_c, dm_c, 0, 4, WIDE)
    product_t(qkv_c[...], w_cq, WIDE // TILE, store_to(n_c, everything))
    for w in range(4):
        rows = slice(64 * w, 64 * w + 64)
        (d,) = norm_grad([xc[rows, :]], [n_c[rows, :].astype(F32)], [coarse_gain[...]], WIDE)
        full = d + dco[rows, :].astype(F32)
        gci[2:10, 8 + 8 * w : 16 + 8 * w, :] = full.reshape(8, 8, WIDE)
        gci_s[0][w] = full[48:].astype(BF16)
    gci_s[1][...] = pieces(full, 6, 2).astype(BF16)
    gci_copies = exchange(15, gci_s, gci_d, (0, 16), (0, 16), False)

    def merge_grad(batch):
        first, last = batch[0][3], batch[-1][3] + batch[-1][2]
        for row, col, count, at in batch:
            n_c[at : at + count, :] = gci[row, 6 + col : 6 + col + count, :].astype(BF16)
        product_t(n_c[first:last, :], w_m, 4 * CH // TILE, store_to(cells, slice(first, last)))
        gains = [merge_gain[:, CH * j : CH * (j + 1)] for j in range(4)]
        for row, col, count, at in batch:
            grads = [cells[at : at + count, CH * j : CH * (j + 1)].astype(F32) for j in range(4)]
            done = norm_grad(merged(row, col, count), grads, gains, 4 * CH)
            for a in range(2):
                for b in range(2):
                    full = spread(cotx, 4 + 2 * row + a, 4 + 2 * col + b, count) + done[2 * a + b]
                    for j in range(4):
                        gf[2 * row + a, j, pl.ds(2 * col + b, count, stride=2), :] = full[:, 128 * j : 128 * j + 128]

    def window(wr, w):
        return jnp.concatenate(
            [gf[8 * wr : 8 * wr + 8, j, aligned(w, 8), :].reshape(64, 128) for j in range(4)], axis=1)
    gt = tok
    def fine_grad(first, count):
        rows = window_rows(first, count)
        for w in range(first, first + count):
            n_f[64 * w : 64 * w + 64, :] = window(w // 8, w % 8).astype(BF16)
        product_t(n_f[rows, :], w_fp, CH // TILE, store_to(m_f, rows))
        attention_grad(qkv_f, p_f, m_f, first, count, CH)
        product_t(qkv_f[rows, :], w_fq, CH // TILE, store_to(n_f, rows))
        for w in range(first, first + count):
            dn = n_f[64 * w : 64 * w + 64, :].astype(F32)
            (d,) = norm_grad([x_window(w)], [dn], [fine_gain[...]], CH)
            full = window(w // 8, w % 8) + d
            r, c = 8 * (w // 8), 8 * (w % 8)
            gt[4 + r : 12 + r, 8 + c : 16 + c, :] = full.reshape(8, 8, CH)
            if w >= 8:
                gt_s[0][w - 8] = full[32:].astype(BF16)
            if w % 8 == 7:
                gt_s[1][32 * (w // 8) : 32 * (w // 8) + 32, :] = pieces(full, 4, 4).astype(BF16)
    for c in cot_copies:
        c.wait_recv()
    for i in range(4):
        for j in range(4):
            cotx[16 + i, j, 0:64, :] = cot_d[0][i, j].astype(F32)
    for i in range(1, 5):
        for j in range(4):
            side = (cot_d[1][i - 1, j] if i < 4 else cot_d[2][0, j]).astype(F32)
            for e in range(4):
                cotx[4 * i + e, j, 64:68, :] = side[4 * e : 4 * e + 4]
    merge_grad(batch_b)
    fine_grad(12, 4)
    gt_first = pltpu.make_async_remote_copy(
        src_ref=gt_s[0].at[4:8], dst_ref=gt_d[0].at[4:8], send_sem=send_sem.at[24], recv_sem=recv_sem.at[24],
        device_id={"lat": down, "lon": lon}, device_id_type=MESH)
    gt_first.start()
    for c in fo_copies:
        c.wait_recv()
    for w in range(8):
        strip = fo_d[0][w].astype(F32)
        for a in range(4):
            full = tok[a, 4 + 8 * w : 12 + 8 * w, :] + strip[8 * a : 8 * a + 8]
            for j in range(4):
                fo[a, j, 8 + 8 * w : 16 + 8 * w, :] = full[:, 128 * j : 128 * j + 128]
    side, tip = fo_d[1][...].astype(F32), fo_d[2][...].astype(F32)
    for a in range(16):
        full = tok[a, 0:4, :] + (tip[4 * a : 4 * a + 4] if a < 4 else side[4 * a - 16 : 4 * a - 12])
        for j in range(4):
            fo[a, j, 4:8, :] = full[:, 128 * j : 128 * j + 128]
    for c in co_copies:
        c.wait_recv()
    for w in range(4):
        strip = co_d[0][w].astype(F32)
        for a in range(4):
            co[a, 8 + 8 * w : 16 + 8 * w, :] = strip[8 * a : 8 * a + 8]
    side, tip = co_d[1][...].astype(F32), co_d[2][...].astype(F32)
    for a in range(4):
        co[a, 4:8, :] = tip[4 * a : 4 * a + 4]
        co[4 + a, 4:8, :] = side[4 * a : 4 * a + 4]
    for i in range(8):
        n_c[32 * i : 32 * i + 32, :] = co[i, 4:36, :].astype(BF16)
    for a in range(2):
        for b in range(2):
            part = 2 * a + b
            def lift(n, carry):
                w = w_e[:, pl.ds(part * CH + n * TILE, TILE)]
                lifted = dot(n_c[...], w)
                for s in range(2):
                    j = 2 * n + s
                    for i in range(8):
                        part_fo = fo[2 * i + a, j, pl.ds(4 + b, 32, stride=2), :]
                        res[2 * i + a, j, pl.ds(b, 32, stride=2), :] = part_fo + lifted[32 * i : 32 * i + 32, 128 * s : 128 * s + 128]
                return carry
            unrolled(0, CH // TILE, lift)
    out_result = [
        pltpu.make_async_copy(res.at[:, j], result.at[:, :, 128 * j : 128 * j + 128], load_sem.at[14 + j])
        for j in range(4)
    ]
    for c in out_result:
        c.start()

    for c in gci_copies:
        c.wait_recv()
    for w in range(4):
        strip = gci_d[0][w].astype(F32)
        for a in range(2):
            gci[a, 8 + 8 * w : 16 + 8 * w, :] = strip[8 * a : 8 * a + 8]
    side, tip = gci_d[1][...].astype(F32), gci_d[2][...].astype(F32)
    for a in range(6):
        gci[2 + a, 6:8, :] = side[2 * a : 2 * a + 2]
    for a in range(2):
        gci[a, 6:8, :] = tip[12 + 2 * a : 14 + 2 * a]
    merge_grad(batch_a)
    fine_grad(7, 5)
    gt_copies = exchange(
        18, (gt_s[0].at[0:4], gt_s[1]), (gt_d[0].at[0:4], gt_d[1], gt_d[2]), (0, 48), (48, 64), False)
    fine_grad(0, 7)
    for i in range(4, ROWS):
        xs[i, 8:64, :] = gt[i, 12:68, :]
    out_grad = [
        pltpu.make_async_copy(xs.at[rows, cols], grad.at[rows, cols], load_sem.at[slot])
        for rows, cols, slot in (
            (pl.ds(4, 12), pl.ds(8, 56), 13), (pl.ds(4, 12), pl.ds(0, 8), 18), (pl.ds(0, 4), pl.ds(0, 64), 19))
    ]
    out_grad[0].start()
    gt_copies.append(gt_first)
    for c in gt_copies:
        c.wait_recv()
    side, tip = gt_d[1][...].astype(F32), gt_d[2][...].astype(F32)
    for a in range(16):
        gt[a, 4:8, :] = tip[4 * a : 4 * a + 4] if a < 4 else side[4 * a - 16 : 4 * a - 12]
    for i in range(4, ROWS):
        xs[i, 0:8, :] = gt[i, 4:12, :]
    out_grad[1].start()
    for w in range(8):
        strip = gt_d[0][w].astype(F32)
        for a in range(4):
            gt[a, 8 + 8 * w : 16 + 8 * w, :] = strip[8 * a : 8 * a + 8]
    for i in range(4):
        xs[i] = gt[i, 4:68, :]
    out_grad[2].start()
    for c in tok_copies + cot_copies + dco_copies + cin_copies + fo_copies + co_copies + gci_copies + gt_copies:
        c.wait_send()
    for c in out_result + out_grad:
        c.wait()


def exchanged(strip, side, edge, corner):
    vmem = pltpu.VMEM
    return (
        (vmem(strip, BF16), vmem(side, BF16)),
        (vmem(strip, BF16), vmem((edge,) + side[1:], BF16), vmem((corner,) + side[1:], BF16)),
    )


def local(
    tokens, fine_gain, fine_qkv, fine_proj, merge_gain, merge_weight,
    coarse_gain, coarse_qkv, coarse_proj, expand_weight, cotangent,
):
    vmem = pltpu.VMEM
    shape = jax.ShapeDtypeStruct((ROWS, COLS, CH), F32)
    hbm = pl.BlockSpec(memory_space=pl.ANY)
    whole = pl.BlockSpec(memory_space=pltpu.VMEM)
    done = pl.pallas_call(
        kernel,
        out_shape=(shape, shape),
        in_specs=[hbm, hbm, whole, whole, whole] + [hbm] * 6,
        out_specs=(hbm, hbm),
        scratch_shapes=[
            vmem((20, 72, CH), F32),
            vmem((20, 4, 72, 128), F32),
            vmem((ROWS, COLS, CH), F32),
            vmem((20, 4, 72, 128), F32),
            vmem((10, 40, WIDE), F32),
            vmem((10, 40, WIDE), F32),
            vmem((12, 40, WIDE), F32),
            vmem((256, WIDE), F32),
            vmem((ROWS, 4, COLS, 128), F32),
            vmem((ROWS, 4, COLS, 128), F32),
            vmem((1024, 3 * CH), BF16),
            vmem((1024, CH), F32),
            vmem((256, 3 * WIDE), BF16),
            vmem((256, WIDE), F32),
            vmem((1024, CH), BF16),
            vmem((1024, CH), BF16),
            vmem((256, 4 * CH), BF16),
            vmem((256, WIDE), BF16),
            vmem((256, WIDE), BF16),
            vmem((256, WIDE), BF16),
            vmem((256, WIDE), BF16),
            vmem((2, 64, GROUP), F32),
            vmem(fine_qkv.shape, BF16),
            vmem(fine_proj.shape, BF16),
            vmem(merge_weight.shape, BF16),
            vmem(coarse_qkv.shape, BF16),
            vmem(coarse_proj.shape, BF16),
            vmem(expand_weight.shape, BF16),
            *exchanged((4, 64, CH), (64, CH), 48, 16),
            *exchanged((4, 4, 64, 128), (4, 4, 16, 128), 3, 1),
            *exchanged((4, 32, WIDE), (32, WIDE), 16, 16),
            *exchanged((2, 32, WIDE), (16, WIDE), 16, 16),
            *exchanged((8, 32, CH), (64, CH), 48, 16),
            *exchanged((4, 32, WIDE), (32, WIDE), 16, 16),
            *exchanged((4, 16, WIDE), (16, WIDE), 16, 16),
            *exchanged((8, 32, CH), (64, CH), 48, 16),
            pltpu.SemaphoreType.DMA((20,)),
            pltpu.SemaphoreType.DMA((25,)),
            pltpu.SemaphoreType.DMA((25,)),
        ],
        compiler_params=pltpu.CompilerParams(
            collective_id=0, has_side_effects=True, vmem_limit_bytes=63 * 1024 * 1024),
    )(
        tokens, cotangent, fine_gain.reshape(1, -1), merge_gain.reshape(1, -1), coarse_gain.reshape(1, -1),
        fine_qkv, fine_proj, merge_weight, coarse_qkv, coarse_proj, expand_weight,
    )
    return pl.pallas_call(
        hand_over,
        out_shape=(shape, shape),
        in_specs=[hbm, hbm],
        out_specs=(hbm, hbm),
        scratch_shapes=[
            pltpu.VMEM((8, 4, COLS, CH), F32), pltpu.SemaphoreType.DMA((8,)), pltpu.SemaphoreType.DMA((8,))],
    )(*done)


def hand_over(result, grad, result_out, grad_out, held, load_sem, store_sem):
    loads, stores = [], []
    for i, (src, dst) in enumerate(((result, result_out), (grad, grad_out))):
        for part in range(4):
            rows, slot = pl.ds(4 * part, 4), 4 * i + part
            loads.append(pltpu.make_async_copy(src.at[rows], held.at[slot], load_sem.at[slot]))
            stores.append(pltpu.make_async_copy(held.at[slot], dst.at[rows], store_sem.at[slot]))
            loads[-1].start()
    for load, store in zip(loads, stores):
        load.wait()
        store.start()
    for store in stores:
        store.wait()


def solution(mesh):
    field = P("lat", "lon", None)
    placed = (field,) + (P(),) * 9 + (field,)
    return jax.shard_map(local, mesh=mesh, in_specs=placed, out_specs=(field, field), check_vma=False)
```
